128 devices in a mesh: gx: 16 (over x, z), gy: 8 (over y, core).
Axes of the slice: x: 4, y: 4, z: 4, core: 2. Of those that a mesh axis runs over, the one named last changes fastest.
Arguments:
- features: bfloat16 [16, 8, 16, 8, 8, 768], P('gx', 'gy'), may hold values from -12 to 12
- voxel_mask: int32 [16, 8, 16, 512], P('gx', 'gy'), may hold values 0 or 1
- occupancy: int32 [32, 16, 8], P('gx', 'gy'), may hold values from -1 to 15, as said below
- send_counts: int32 [8, 16, 16], P('gy'), may hold values from 0 to 1, as said below
- weight_one: bfloat16 [27, 96, 128], replicated, may hold values from -0.125 to 0.125
- bias_one: float32 [128], replicated, may hold values from -3 to 3
- weight_two: bfloat16 [27, 128, 128], replicated, may hold values from -0.109375 to 0.109375
- bias_two: float32 [128], replicated, may hold values from -3 to 3
- cotangent: bfloat16 [16, 8, 8, 8, 8, 1024], P('gx', 'gy'), may hold values from -12 to 12
Outputs:
- result: bfloat16 [16, 8, 8, 8, 8, 1024], P('gx', 'gy')
- grad_one: float32 [27, 96, 128], replicated
- grad_two: float32 [27, 128, 128], replicated
The draws below stay inside these ranges and needn't reach their ends.
Inputs may be any that keep to these rules, and one draw needn't show every extreme that they name: `occupancy`: A device's active bricks fill its slots 0 to n - 1 with n at most 16; in every row of tiles along gx the active bricks average 8 per device, and some device holds exactly 16. Row d of send_counts[r] sums to that device's active bricks; every column sums to exactly 8.
All inputs are finite; a program needn't handle non-finite values. No bound on the sum of `voxel_mask` on one device may be relied on, other than what follows from the above.
Results may differ from the reference program's by a relative error of at most 0.0067.
Values may be sent and summed in bfloat16 or wider, within the bound.
A program may use at most 192 MiB of HBM per device.

```python
import math
import jax
import jax.numpy as jnp
from jax import lax

C_IN = 96
C_MID = 128
C_OUT = 128
TX = 2
TY = 2
TZ = 8
WORK = 8
SLOTS = 16
CAP = 1
BX = 32
BY = 16
N_GX = 16
N_GY = 8


def brick_counts(key):
    key = jax.random.fold_in(key, 101)

    def one_row(row_key):
        order = jax.random.permutation(jax.random.fold_in(row_key, 1), N_GX)
        spread = jax.random.randint(jax.random.fold_in(row_key, 2), (N_GX // 2,), 1 - WORK, WORK)
        spread = spread.at[0].set(WORK)
        counts = jnp.zeros((N_GX,), jnp.int32)
        counts = counts.at[order[0::2]].set(WORK + spread)
        return counts.at[order[1::2]].set(WORK - spread)
    return jax.vmap(one_row)(jax.random.split(key, N_GY))


def scaled_field(key, shape, channels, lowest, ratio):
    base_key, scale_key = jax.random.split(key)
    normal_part = jnp.clip(jax.random.normal(base_key, shape, jnp.float32), -4.0, 4.0)
    base = normal_part
    logs = jax.random.uniform(scale_key, (channels,), jnp.float32, math.log(lowest), math.log(lowest * ratio))
    return (base * jnp.tile(jnp.exp(logs), shape[-1] // channels)).astype(jnp.bfloat16)


def draw_occupancy(key, part):
    counts = brick_counts(key)
    key = jax.random.fold_in(key, 7)
    places = TX * TY * TZ

    def one_tile(index):
        order = jax.random.permutation(jax.random.fold_in(key, index), places)
        rank = jnp.argsort(order).astype(jnp.int32)
        count = counts[index % N_GY, index // N_GY]
        return jnp.where(rank < count, rank, -1).astype(jnp.int32)
    tiles = jax.vmap(one_tile)(jnp.arange(N_GX * N_GY, dtype=jnp.int32))
    tiles = tiles.reshape(N_GX, N_GY, TX, TY, TZ).transpose(0, 2, 1, 3, 4)
    return tiles.reshape(TX * N_GX, TY * N_GY, TZ)


def draw_send_counts(key, part):
    counts = brick_counts(key)
    key = jax.random.fold_in(key, 11)
    lanes = jnp.arange(SLOTS, dtype=jnp.int32)
    peers = jnp.arange(N_GX, dtype=jnp.int32)

    def one_row(row_key, row):
        workers = jax.random.permutation(row_key, N_GX).astype(jnp.int32)
        offsets = jnp.cumsum(row) - row
        target = workers[(offsets[:, None] + lanes[None, :]) % N_GX]
        used = lanes[None, :] < row[:, None]
        hits = used[:, :, None] & (target[:, :, None] == peers[None, None, :])
        return jnp.sum(hits.astype(jnp.int32), axis=1)
    return jax.vmap(one_row)(jax.random.split(key, N_GY), counts)


def draw_features(key, part):
    key = jax.random.fold_in(key, 23)
    shape = (N_GX, N_GY, SLOTS, 8, 8, 8 * C_IN)
    return scaled_field(key, shape, C_IN, 0.3, 10.0)


def draw_cotangent(key, part):
    key = jax.random.fold_in(key, 29)
    shape = (N_GX, N_GY, WORK, 8, 8, 8 * C_OUT)
    return scaled_field(key, shape, C_OUT, 0.3, 10.0)


def set_ends(values, own_key, smallest, largest):
    longest = values.shape.index(max(values.shape))
    spots = []
    for shift in (0, 1):
        where = [jax.random.randint(jax.random.fold_in(own_key, axis), (), 0, length) for axis, length in enumerate(values.shape)]
        where[longest] = (where[longest] + shift) % values.shape[longest]
        spots.append(tuple(where))
    return values.at[spots[0]].set(smallest).at[spots[1]].set(largest)


def normal_values(key, extent, deviation, limit, kind=jnp.bfloat16):
    drawn = jax.random.normal(key, extent, jnp.float32) * deviation
    return jnp.minimum(jnp.maximum(drawn, -limit), limit).astype(kind)


def setup_inputs(seed: int = 0) -> dict:
    streams_of = jax.random.split(jax.random.key(seed), 10)
    features = draw_features(jax.random.fold_in(streams_of[9], 71), 0)
    voxel_mask = set_ends((jax.random.randint(streams_of[1], (N_GX, N_GY, SLOTS, 512), 0, 3) < 2).astype(jnp.int32), jax.random.fold_in(streams_of[1], 1), 0, 1)
    occupancy = draw_occupancy(jax.random.fold_in(streams_of[9], 71), 0)
    send_counts = draw_send_counts(jax.random.fold_in(streams_of[9], 71), 0)
    weight_one = normal_values(streams_of[4], (27, C_IN, C_MID), (27 * C_IN) ** -0.5, 0.125)
    bias_one = normal_values(streams_of[5], (C_MID,), 0.5, 3.0, jnp.float32)
    weight_two = normal_values(streams_of[6], (27, C_MID, C_OUT), (27 * C_MID) ** -0.5, 0.109375)
    bias_two = normal_values(streams_of[7], (C_OUT,), 0.5, 3.0, jnp.float32)
    cotangent = draw_cotangent(jax.random.fold_in(streams_of[9], 71), 0)
    return {"features": features, "voxel_mask": voxel_mask, "occupancy": occupancy, "send_counts": send_counts, "weight_one": weight_one, "bias_one": bias_one, "weight_two": weight_two, "bias_two": bias_two, "cotangent": cotangent}


OFFSETS = [(a, b, c) for a in range(3) for b in range(3) for c in range(3)]
PARTS = [(slice(0, 1), slice(9, 10)), (slice(0, 8), slice(1, 9)), (slice(7, 8), slice(0, 1))]

def silu_slope(value):
    sig = jax.nn.sigmoid(value)
    return sig * (1.0 + value * (1.0 - sig))

def gather_taps(padded, span):
    return jnp.concatenate([padded[a:a + span, b:b + span, c:c + span] for a, b, c in OFFSETS], axis=-1)

def mirror_taps(padded):
    return jnp.concatenate([padded[2 - a:12 - a, 2 - b:12 - b, 2 - c:12 - c] for a, b, c in OFFSETS], axis=-1)

def assemble(bricks, around):
    blocks = bricks[around.reshape(-1)].reshape(3, 3, 3, 8, 8, 8, bricks.shape[-1])
    canvas = blocks.transpose(0, 3, 1, 4, 2, 5, 6).reshape(24, 24, 24, bricks.shape[-1])
    return canvas[7:17, 7:17, 7:17]

def source_map(send_counts):
    lanes = jnp.arange(CAP, dtype=jnp.int32)
    start = (jnp.cumsum(send_counts, axis=2) - send_counts).astype(jnp.int32)
    valid = lanes[None, None, None, :] < send_counts[..., None]
    valid = valid.transpose(0, 2, 1, 3).reshape(N_GY, N_GX, N_GX * CAP)
    first_slot = (start[..., None] + lanes).transpose(0, 2, 1, 3).reshape(N_GY, N_GX, N_GX * CAP).astype(jnp.int32)
    source = jnp.repeat(jnp.arange(N_GX, dtype=jnp.int32), CAP)
    rank = (jnp.cumsum(valid.astype(jnp.int32), axis=2) - 1).astype(jnp.int32)
    wanted = jnp.arange(WORK, dtype=jnp.int32)[:, None]
    hits = valid[..., None, :] & (rank[..., None, :] == wanted)
    sender = lax.optimization_barrier(jnp.sum(jnp.where(hits, source, 0), axis=-1)).astype(jnp.int32)
    chosen = lax.optimization_barrier(jnp.sum(jnp.where(hits, first_slot[..., None, :], 0), axis=-1)).astype(jnp.int32)
    row_index = jnp.arange(N_GY, dtype=jnp.int32)[:, None, None]
    global_slot = (sender * N_GY + row_index) * SLOTS + chosen
    return global_slot.transpose(1, 0, 2).astype(jnp.int32)

def normalized(grad):
    return grad * lax.rsqrt(jnp.mean(grad * grad) + 1e-05)

def reference(features, voxel_mask, occupancy, send_counts, weight_one, bias_one, weight_two, bias_two, cotangent):
    total = N_GX * N_GY * SLOTS
    mask_all = voxel_mask.reshape(total, 8, 8, 8, 1).astype(jnp.bfloat16)
    inputs = features.reshape(total, 8, 8, 8, C_IN) * mask_all
    owner_x = (jnp.arange(BX, dtype=jnp.int32) // TX)[:, None, None]
    owner_y = (jnp.arange(BY, dtype=jnp.int32) // TY)[None, :, None]
    slot_grid = jnp.where(occupancy >= 0, (owner_x * N_GY + owner_y) * SLOTS + occupancy, total).astype(jnp.int32)
    table = jnp.pad(slot_grid, 1, constant_values=total)
    grids = jnp.meshgrid(jnp.arange(BX, dtype=jnp.int32), jnp.arange(BY, dtype=jnp.int32), jnp.arange(TZ, dtype=jnp.int32), indexing='ij')
    coords = jnp.stack(grids, -1).reshape(-1, 3)
    place = jnp.zeros((total + 1, 3), jnp.int32).at[slot_grid.reshape(-1)].set(coords)
    alive = jnp.zeros((total + 1,), jnp.float32).at[slot_grid.reshape(-1)].set(1.0)[:total]
    slots_all = jnp.arange(total, dtype=jnp.int32)

    def neighbours(index):
        spot = place[index]
        return lax.dynamic_slice(table, (spot[0], spot[1], spot[2]), (3, 3, 3))

    def keep_of(index):
        return mask_all[index].reshape(512, 1).astype(jnp.float32) * alive[index]
    input_table = jnp.concatenate([inputs, jnp.zeros((1, 8, 8, 8, C_IN), jnp.bfloat16)], 0)
    flat_one = weight_one.reshape(27 * C_IN, C_MID)

    def first(index):
        padded = assemble(input_table, neighbours(index))
        columns = gather_taps(padded, 8).reshape(512, 27 * C_IN)
        linear = jnp.dot(columns, flat_one, preferred_element_type=jnp.float32) + bias_one
        keep = keep_of(index)
        hidden_brick = (keep * jax.nn.silu(linear)).astype(jnp.bfloat16).reshape(8, 8, 8, C_MID)
        gate_brick = (keep * silu_slope(linear)).astype(jnp.bfloat16).reshape(8, 8, 8, C_MID)
        return (hidden_brick, gate_brick)
    hidden, gate_one = lax.map(first, slots_all)
    slope_source = source_map(send_counts).reshape(-1)
    slopes_in = jnp.zeros((total + 1, 8, 8, 8 * C_OUT), jnp.bfloat16).at[slope_source].set(cotangent.reshape(-1, 8, 8, 8 * C_OUT))[:total]
    hidden_table = jnp.concatenate([hidden, jnp.zeros((1, 8, 8, 8, C_MID), jnp.bfloat16)], 0)
    flat_two = weight_two.reshape(27 * C_MID, C_OUT)
    mirrored = weight_two.transpose(0, 2, 1).reshape(27 * C_OUT, C_MID)

    def second(carry, index):
        padded = assemble(hidden_table, neighbours(index))
        columns = gather_taps(padded, 8).reshape(512, 27 * C_MID)
        linear = jnp.dot(columns, flat_two, preferred_element_type=jnp.float32) + bias_two
        keep = keep_of(index)
        output = (keep * jax.nn.silu(linear)).astype(jnp.bfloat16)
        slope_live = (slopes_in[index].reshape(512, C_OUT).astype(jnp.float32) * keep * silu_slope(linear)).astype(jnp.bfloat16)
        carry = carry + jnp.dot(columns.T, slope_live, preferred_element_type=jnp.float32)
        wide = jnp.pad(slope_live.reshape(8, 8, 8, C_OUT), ((2, 2), (2, 2), (2, 2), (0, 0)))
        spread_columns = mirror_taps(wide).reshape(1000, 27 * C_OUT)
        spread = jnp.dot(spread_columns, mirrored, preferred_element_type=jnp.float32).astype(jnp.bfloat16)
        return (carry, (output.reshape(8, 8, 8 * C_OUT), spread.reshape(10, 10, 10, C_MID)))
    grad_two, (outputs, spreads) = lax.scan(second, jnp.zeros((27 * C_MID, C_OUT), jnp.float32), slots_all)
    spread_table = jnp.concatenate([spreads, jnp.zeros((1, 10, 10, 10, C_MID), jnp.bfloat16)], 0)

    def first_back(index):
        blocks = spread_table[neighbours(index).reshape(-1)]
        gathered = jnp.zeros((8, 8, 8, C_MID), jnp.float32)
        for number, (a, b, c) in enumerate(OFFSETS):
            (take_a, from_a), (take_b, from_b), (take_c, from_c) = (PARTS[a], PARTS[b], PARTS[c])
            gathered = gathered.at[take_a, take_b, take_c].add(blocks[number][from_a, from_b, from_c].astype(jnp.float32))
        return (gathered * gate_one[index].astype(jnp.float32)).astype(jnp.bfloat16)
    slope_one = lax.map(first_back, slots_all)

    def first_weights(carry, index):
        padded = assemble(input_table, neighbours(index))
        columns = gather_taps(padded, 8).reshape(512, 27 * C_IN)
        return (carry + jnp.dot(columns.T, slope_one[index].reshape(512, C_MID), preferred_element_type=jnp.float32), None)
    grad_one, _ = lax.scan(first_weights, jnp.zeros((27 * C_IN, C_MID), jnp.float32), slots_all)
    result = outputs[slope_source].reshape(N_GX, N_GY, WORK, 8, 8, 8 * C_OUT)
    return (result, normalized(grad_one).reshape(27, C_IN, C_MID), normalized(grad_two).reshape(27, C_MID, C_OUT))
```

```python
import functools

import jax
import jax.numpy as jnp
from jax import lax
from jax.experimental import pallas as pl
from jax.experimental.pallas import tpu as pltpu
from jax.sharding import PartitionSpec as P

MESH = pl.DeviceIdType.MESH
F32 = jnp.float32
BF16 = jnp.bfloat16
C = 128
BRICK = 8 * C
LINE = 8 * BRICK
WIDE = LINE + 2 * C
PATCH = BRICK + 2 * C
LIMIT = 60 * 1024 * 1024

VMEM = pl.BlockSpec(memory_space=pltpu.VMEM)
SMEM = pl.BlockSpec(memory_space=pltpu.SMEM)
ANY = pl.BlockSpec(memory_space=pl.ANY)

VOLUME = jax.ShapeDtypeStruct((16, 2, 8, LINE), BF16)
FACES = jax.ShapeDtypeStruct((2, 2, 8, LINE), BF16)
CORNERS = jax.ShapeDtypeStruct((4, 8, BRICK), BF16)


def coords(place):
    return place // 16, lax.rem(place // 8, 2), lax.rem(place, 8)


def put(vol, faces, spot, lane, value):
    xb, yb, zb = spot
    lanes = pl.ds(pl.multiple_of(zb * BRICK + lane, C), value.shape[2])
    vol[pl.ds(xb * 8, 8), yb, :, lanes] = value.astype(BF16)
    row = jnp.where(yb == 0, value[:, 0, :], value[:, 7, :])
    faces[yb, xb, :, lanes] = row.astype(BF16)


def put_corners(faces, corners):
    for side_y in range(2):
        for side_x in range(2):
            face = faces[side_y, side_x].astype(F32)
            row = face[7 * side_x : 7 * side_x + 1]
            rows = [row[:, z * BRICK : (z + 1) * BRICK] for z in range(8)]
            corners[2 * side_y + side_x] = jnp.concatenate(rows, axis=0).astype(BF16)


def volume_kernel(info, feat, mask, vol, faces, corners):
    vol[...] = jnp.zeros(vol.shape, BF16)
    faces[...] = jnp.zeros(faces.shape, BF16)
    c_in = feat.shape[3] // 8

    def step(place, _):
        slot = info[place]

        @pl.when(slot >= 0)
        def _():
            rows = feat[slot].astype(F32)
            keep = mask[slot].reshape(8, 8, 8)
            pieces = []
            for w in range(8):
                pieces.append(rows[:, :, w * c_in : (w + 1) * c_in] * keep[:, :, w : w + 1])
                pieces.append(jnp.zeros((8, 8, C - c_in), F32))
            put(vol, faces, coords(place), 0, jnp.concatenate(pieces, axis=2))

        return 0

    lax.fori_loop(0, 32, step, 0)
    put_corners(faces, corners)


def halo_kernel(vol, faces, corners, x_halo, y_halo, c_halo, send_sem, recv_sem):
    nx, ny = lax.axis_size("gx"), lax.axis_size("gy")
    x, y = lax.axis_index("gx"), lax.axis_index("gy")
    left, right = lax.rem(x + nx - 1, nx), lax.rem(x + 1, nx)
    down, up = lax.rem(y + ny - 1, ny), lax.rem(y + 1, ny)
    plan = [
        (vol.at[0], x_halo.at[1], (left, y)),
        (vol.at[15], x_halo.at[0], (right, y)),
        (faces.at[0], y_halo.at[1], (x, down)),
        (faces.at[1], y_halo.at[0], (x, up)),
        (corners.at[0], c_halo.at[3], (left, down)),
        (corners.at[1], c_halo.at[2], (right, down)),
        (corners.at[2], c_halo.at[1], (left, up)),
        (corners.at[3], c_halo.at[0], (right, up)),
    ]
    barrier = pltpu.get_barrier_semaphore()
    for _, _, device in plan:
        pl.semaphore_signal(barrier, inc=1, device_id=device, device_id_type=MESH)
    pl.semaphore_wait(barrier, len(plan))
    copies = []
    for number, (source, target, device) in enumerate(plan):
        copy = pltpu.make_async_remote_copy(
            src_ref=source,
            dst_ref=target,
            send_sem=send_sem.at[number],
            recv_sem=recv_sem.at[number],
            device_id=device,
            device_id_type=MESH,
        )
        copy.start()
        copies.append(copy)
    for copy in copies:
        copy.wait()


def halo_exchange(vol, faces, corners, number):
    return pl.pallas_call(
        halo_kernel,
        out_shape=(jax.ShapeDtypeStruct((2, 2, 8, LINE), BF16), FACES, CORNERS),
        in_specs=[ANY] * 3,
        out_specs=(ANY,) * 3,
        scratch_shapes=[pltpu.SemaphoreType.DMA((8,)), pltpu.SemaphoreType.DMA((8,))],
        compiler_params=pltpu.CompilerParams(collective_id=number, has_side_effects=True),
        name="halo",
    )(vol, faces, corners)


def load_volume(info, own, x_halo, y_halo, c_halo, wide, sems):
    inner = pl.ds(C, LINE)
    copies = [
        pltpu.make_async_copy(own, wide.at[pl.ds(1, 16), pl.ds(1, 2), :, inner], sems.at[0]),
        pltpu.make_async_copy(x_halo.at[0], wide.at[0, pl.ds(1, 2), :, inner], sems.at[1]),
        pltpu.make_async_copy(x_halo.at[1], wide.at[17, pl.ds(1, 2), :, inner], sems.at[2]),
    ]
    for copy in copies:
        copy.start()
    margin = jnp.zeros((18, 4, 8, C), BF16)
    wide[:, :, :, 0:C] = margin
    wide[:, :, :, C + LINE : WIDE] = margin
    for side in range(2):
        block = 3 * side
        inside_y = info[34 + side] > 0
        for half in range(2):
            face = jnp.where(inside_y, y_halo[side, half].astype(F32), 0.0)
            for row in range(8):
                wide[1 + 8 * half + row, block, :, inner] = jnp.broadcast_to(
                    face[row : row + 1], (8, LINE)
                ).astype(BF16)
        for end in range(2):
            inside = inside_y & (info[32 + end] > 0)
            corner = jnp.where(inside, c_halo[2 * side + end].astype(F32), 0.0)
            for z in range(8):
                wide[17 * end, block, :, pl.ds(C + z * BRICK, BRICK)] = jnp.broadcast_to(
                    corner[z : z + 1], (8, BRICK)
                ).astype(BF16)
    for copy in copies:
        copy.wait()
    for end in range(2):

        @pl.when(info[32 + end] == 0)
        def _():
            wide[17 * end, 1:3, :, inner] = jnp.zeros((2, 8, LINE), BF16)


def cut_patch(wide, spot, even, odd):
    xb, yb, zb = spot
    lanes = pl.ds(pl.multiple_of(zb * BRICK, C), PATCH)
    rows = pl.ds(xb * 8, 10)
    before = wide[rows, yb, :, lanes].astype(F32)
    here = wide[rows, yb + 1, :, lanes].astype(F32)
    after = wide[rows, yb + 2, :, lanes].astype(F32)
    line = lax.broadcasted_iota(jnp.int32, here.shape, 1)
    shifts = [
        pltpu.roll(jnp.where(line == 7, before, here), 1, 1),
        here,
        pltpu.roll(jnp.where(line == 0, after, here), 7, 1),
    ]
    for b in range(3):
        even[b] = shifts[b].reshape(80, PATCH).astype(BF16)
        odd[b] = shifts[b][1:9].reshape(64, PATCH).astype(BF16)


def window(even, odd, a, b):
    parts = []
    for j in range(4):
        lanes = pl.ds(2 * C * j, 4 * C)
        parts.append(odd[b, :, lanes] if a == 1 else even[b, pl.ds(8 * a, 64), lanes])
    return jnp.concatenate(parts, axis=0)


def fill_band(band, taps):
    depth = taps.shape[1]
    band[...] = jnp.zeros(band.shape, BF16)
    for tap in range(9):
        for c in range(3):
            for o in range(2):
                band[tap, pl.ds((c + o) * C, depth), pl.ds(o * C, C)] = taps[3 * tap + c]


def convolve(even, odd, band):
    total = jnp.zeros((256, 2 * C), F32)
    for a in range(3):
        for b in range(3):
            total = total + jnp.dot(
                window(even, odd, a, b), band[3 * a + b], preferred_element_type=F32
            )
    return total


def add_taps(sums, slopes, even, odd):
    turned = slopes.T.astype(BF16)
    for a in range(3):
        for b in range(3):
            sums[3 * a + b] += jnp.dot(
                turned, window(even, odd, a, b), preferred_element_type=F32
            )


def gather_taps(sums, grad):
    depth = grad.shape[1]
    for tap in range(9):
        for c in range(3):
            part = (
                sums[tap, 0:C, c * C : (c + 1) * C]
                + sums[tap, C : 2 * C, (c + 1) * C : (c + 2) * C]
            )
            grad[3 * tap + c] = part.T[0:depth]


def spread_mask(keep):
    blocks = []
    for j in range(4):
        pair = [jnp.broadcast_to(keep[:, 2 * j + o : 2 * j + o + 1], (64, C)) for o in range(2)]
        blocks.append(jnp.concatenate(pair, axis=1))
    return jnp.concatenate(blocks, axis=0)


def sigmoid(value):
    return 1.0 / (1.0 + jnp.exp(-value))


def first_kernel(
    info, own, x_halo, y_halo, c_halo, mask, taps, bias,
    vol, faces, corners, gates,
    wide, band, even, odd, sems,
):
    load_volume(info, own, x_halo, y_halo, c_halo, wide, sems)
    fill_band(band, taps)
    vol[...] = jnp.zeros(vol.shape, BF16)
    faces[...] = jnp.zeros(faces.shape, BF16)

    def step(place, _):
        slot = info[place]

        @pl.when(slot >= 0)
        def _():
            spot = coords(place)
            cut_patch(wide, spot, even, odd)
            linear = convolve(even, odd, band) + bias[...]
            keep = spread_mask(mask[slot])
            sig = sigmoid(linear)
            hidden = keep * (linear * sig)
            gates[slot] = (keep * (sig * (1.0 + linear * (1.0 - sig)))).astype(BF16)
            for j in range(4):
                piece = hidden[64 * j : 64 * j + 64].reshape(8, 8, 2 * C)
                put(vol, faces, spot, 2 * C * j, piece)

        return 0

    lax.fori_loop(0, 32, step, 0)
    put_corners(faces, corners)


def second_kernel(
    info, own, x_halo, y_halo, c_halo, mask, taps, bias, cots,
    vol, faces, corners, results, grad,
    wide, band, even, odd, sums, sems,
):
    load_volume(info, own, x_halo, y_halo, c_halo, wide, sems)
    fill_band(band, taps)
    vol[...] = jnp.zeros(vol.shape, BF16)
    faces[...] = jnp.zeros(faces.shape, BF16)
    sums[...] = jnp.zeros(sums.shape, F32)

    def step(place, _):
        slot = info[place]

        @pl.when(slot >= 0)
        def _():
            spot = coords(place)
            worker = info[36 + slot]
            cut_patch(wide, spot, even, odd)
            linear = convolve(even, odd, band) + bias[...]
            keep = spread_mask(mask[slot])
            sig = sigmoid(linear)
            output = keep * (linear * sig)
            slope = keep * (sig * (1.0 + linear * (1.0 - sig)))
            slopes = []
            for j in range(4):
                rows = slice(64 * j, 64 * j + 64)
                lanes = pl.ds(2 * C * j, 2 * C)
                results[worker, :, :, lanes] = output[rows].reshape(8, 8, 2 * C).astype(BF16)
                piece = cots[worker, :, :, lanes].astype(F32).reshape(64, 2 * C) * slope[rows]
                slopes.append(piece)
                put(vol, faces, spot, 2 * C * j, piece.reshape(8, 8, 2 * C))
            add_taps(sums, jnp.concatenate(slopes, axis=0), even, odd)

        return 0

    lax.fori_loop(0, 32, step, 0)
    put_corners(faces, corners)
    gather_taps(sums, grad)


def third_kernel(
    info, own, x_halo, y_halo, c_halo, own_in, x_halo_in, y_halo_in, c_halo_in, gates, taps,
    grad,
    wide, wide_in, band, even, odd, even_in, odd_in, sums, sems, sems_in,
):
    load_volume(info, own_in, x_halo_in, y_halo_in, c_halo_in, wide_in, sems_in)
    load_volume(info, own, x_halo, y_halo, c_halo, wide, sems)
    fill_band(band, taps)
    sums[...] = jnp.zeros(sums.shape, F32)

    def step(place, _):
        slot = info[place]

        @pl.when(slot >= 0)
        def _():
            spot = coords(place)
            cut_patch(wide, spot, even, odd)
            cut_patch(wide_in, spot, even_in, odd_in)
            back = convolve(even, odd, band)
            add_taps(sums, back * gates[slot].astype(F32), even_in, odd_in)

        return 0

    lax.fori_loop(0, 32, step, 0)
    gather_taps(sums, grad)


WIDE_SCRATCH = pltpu.VMEM((18, 4, 8, WIDE), BF16)
BAND_SCRATCH = pltpu.VMEM((9, 4 * C, 2 * C), BF16)
EVEN_SCRATCH = pltpu.VMEM((3, 80, PATCH), BF16)
ODD_SCRATCH = pltpu.VMEM((3, 64, PATCH), BF16)
SUMS_SCRATCH = pltpu.VMEM((9, 2 * C, 4 * C), F32)
SEMS = pltpu.SemaphoreType.DMA((3,))
PARAMS = pltpu.CompilerParams(vmem_limit_bytes=LIMIT)


def normalized(grad):
    return grad * lax.rsqrt(jnp.mean(grad * grad) + 1e-05)


def body(
    features,
    voxel_mask,
    occupancy,
    send_counts,
    weight_one,
    bias_one,
    weight_two,
    bias_two,
    cotangent,
):
    x, y = lax.axis_index("gx"), lax.axis_index("gy")
    nx, ny = lax.axis_size("gx"), lax.axis_size("gy")
    c_in = weight_one.shape[1]
    lanes = jnp.arange(16, dtype=jnp.int32)
    table = send_counts[0]
    outgoing = table[x]
    incoming = table[:, x]
    start = jnp.cumsum(outgoing) - outgoing
    rank = jnp.cumsum(incoming) - incoming
    hits = (start[None, :] == lanes[:, None]) & (outgoing[None, :] > 0)
    worker = jnp.sum(jnp.where(hits, lanes[None, :], 0), axis=1)
    edges = jnp.stack([x > 0, x < nx - 1, y > 0, y < ny - 1]).astype(jnp.int32)
    info = jnp.concatenate([occupancy.reshape(32), edges, worker.astype(jnp.int32)])

    cots = lax.all_to_all(
        cotangent[0, 0][jnp.minimum(rank, 7)], "gx", split_axis=0, concat_axis=0, tiled=True
    )
    mask = voxel_mask[0, 0].reshape(16, 64, 8).astype(F32)
    vol_in = pl.pallas_call(
        volume_kernel,
        out_shape=(VOLUME, FACES, CORNERS),
        in_specs=[SMEM, VMEM, VMEM],
        out_specs=(VMEM,) * 3,
        compiler_params=PARAMS,
        name="volume",
    )(info, features[0, 0], mask)
    halo_in = halo_exchange(*vol_in, 0)

    *hidden, gates = pl.pallas_call(
        first_kernel,
        out_shape=(VOLUME, FACES, CORNERS, jax.ShapeDtypeStruct((16, 256, 2 * C), BF16)),
        in_specs=[SMEM, ANY, ANY, VMEM, VMEM, VMEM, VMEM, VMEM],
        out_specs=(VMEM,) * 4,
        scratch_shapes=[WIDE_SCRATCH, BAND_SCRATCH, EVEN_SCRATCH, ODD_SCRATCH, SEMS],
        compiler_params=PARAMS,
        name="first",
    )(info, vol_in[0], *halo_in, mask, weight_one, jnp.tile(bias_one, 2)[None])
    halo_mid = halo_exchange(*hidden, 1)

    *slopes, results, grad_two = pl.pallas_call(
        second_kernel,
        out_shape=(
            VOLUME,
            FACES,
            CORNERS,
            jax.ShapeDtypeStruct((16, 8, 8, BRICK), BF16),
            jax.ShapeDtypeStruct(weight_two.shape, F32),
        ),
        in_specs=[SMEM, ANY, ANY, VMEM, VMEM, VMEM, VMEM, VMEM, VMEM],
        out_specs=(VMEM,) * 5,
        scratch_shapes=[
            WIDE_SCRATCH, BAND_SCRATCH, EVEN_SCRATCH, ODD_SCRATCH, SUMS_SCRATCH, SEMS,
        ],
        compiler_params=PARAMS,
        name="second",
    )(info, hidden[0], *halo_mid, mask, weight_two, jnp.tile(bias_two, 2)[None], cots)
    arrived = lax.all_to_all(results, "gx", split_axis=0, concat_axis=0, tiled=True)
    grad_two = lax.psum(grad_two, ("gx", "gy"))
    halo_back = halo_exchange(*slopes, 2)

    mirrored = weight_two[::-1].transpose(0, 2, 1)
    grad_one = pl.pallas_call(
        third_kernel,
        out_shape=jax.ShapeDtypeStruct(weight_one.shape, F32),
        in_specs=[SMEM, ANY, ANY, VMEM, VMEM, ANY, ANY, VMEM, VMEM, VMEM, VMEM],
        out_specs=VMEM,
        scratch_shapes=[
            WIDE_SCRATCH, WIDE_SCRATCH, BAND_SCRATCH, EVEN_SCRATCH, ODD_SCRATCH,
            EVEN_SCRATCH, ODD_SCRATCH, SUMS_SCRATCH, SEMS, SEMS,
        ],
        compiler_params=PARAMS,
        name="third",
    )(info, slopes[0], *halo_back, vol_in[0], *halo_in, gates, mirrored)
    grad_one = lax.psum(grad_one, ("gx", "gy"))

    wanted = jnp.arange(8, dtype=jnp.int32)
    from_whom = (rank[None, :] == wanted[:, None]) & (incoming[None, :] > 0)
    sender = jnp.sum(jnp.where(from_whom, lanes[None, :], 0), axis=1)
    return (arrived[sender][None, None], normalized(grad_one), normalized(grad_two))


def solution(mesh):
    placed = (
        P("gx", "gy", None, None, None, None),
        P("gx", "gy", None, None),
        P("gx", "gy", None),
        P("gy", None, None),
        P(),
        P(),
        P(),
        P(),
        P("gx", "gy", None, None, None, None),
    )
    return jax.shard_map(
        body,
        mesh=mesh,
        in_specs=placed,
        out_specs=(P("gx", "gy", None, None, None, None), P(), P()),
        check_vma=False,
    )
```

```python
import functools

import jax
import jax.numpy as jnp
from jax import lax
from jax.experimental import pallas as pl
from jax.experimental.pallas import tpu as pltpu
from jax.sharding import PartitionSpec as P

MESH = pl.DeviceIdType.MESH
F32 = jnp.float32
BF16 = jnp.bfloat16
GROUP = 2
C = 128
BRICK = 8 * C
LINE = 8 * BRICK
WIDE = LINE + 2 * C
PATCH = BRICK + 2 * C
LIMIT = 60 * 1024 * 1024

VMEM = pl.BlockSpec(memory_space=pltpu.VMEM)
SMEM = pl.BlockSpec(memory_space=pltpu.SMEM)
ANY = pl.BlockSpec(memory_space=pl.ANY)

VOLUME = jax.ShapeDtypeStruct((16, 2, 8, LINE), BF16)
FACES = jax.ShapeDtypeStruct((2, 2, 8, LINE), BF16)
CORNERS = jax.ShapeDtypeStruct((4, 8, BRICK), BF16)


def coords(place):
    return place // 16, lax.rem(place // 8, 2), lax.rem(place, 8)


def put(vol, faces, spot, lane, value):
    xb, yb, zb = spot
    lanes = pl.ds(pl.multiple_of(zb * BRICK + lane, C), value.shape[2])
    vol[pl.ds(xb * 8, 8), yb, :, lanes] = value.astype(BF16)
    row = jnp.where(yb == 0, value[:, 0, :], value[:, 7, :])
    faces[yb, xb, :, lanes] = row.astype(BF16)


def put_corners(faces, corners):
    for side_y in range(2):
        for side_x in range(2):
            face = faces[side_y, side_x].astype(F32)
            row = face[7 * side_x : 7 * side_x + 1]
            rows = [row[:, z * BRICK : (z + 1) * BRICK] for z in range(8)]
            corners[2 * side_y + side_x] = jnp.concatenate(rows, axis=0).astype(BF16)


def volume_kernel(info, feat, mask, vol, faces, corners, order):
    def sort(place, counts):
        active, empty = counts
        live = info[place] >= 0
        order[jnp.where(live, active, 31 - empty)] = place
        one = live.astype(jnp.int32)
        return active + one, empty + 1 - one

    order[32] = lax.fori_loop(0, 32, sort, (0, 0))[0]
    vol[...] = jnp.zeros(vol.shape, BF16)
    faces[...] = jnp.zeros(faces.shape, BF16)
    c_in = feat.shape[3] // 8

    def step(place, _):
        slot = info[place]

        @pl.when(slot >= 0)
        def _():
            rows = feat[slot].astype(F32)
            keep = mask[slot].reshape(8, 8, 8)
            pieces = []
            for w in range(8):
                pieces.append(rows[:, :, w * c_in : (w + 1) * c_in] * keep[:, :, w : w + 1])
                pieces.append(jnp.zeros((8, 8, C - c_in), F32))
            put(vol, faces, coords(place), 0, jnp.concatenate(pieces, axis=2))

        return 0

    lax.fori_loop(0, 32, step, 0)
    put_corners(faces, corners)


def halo_kernel(vol, faces, corners, x_halo, y_halo, c_halo, send_sem, recv_sem):
    nx, ny = lax.axis_size("gx"), lax.axis_size("gy")
    x, y = lax.axis_index("gx"), lax.axis_index("gy")
    left, right = lax.rem(x + nx - 1, nx), lax.rem(x + 1, nx)
    down, up = lax.rem(y + ny - 1, ny), lax.rem(y + 1, ny)
    plan = [
        (vol.at[0], x_halo.at[1], (left, y)),
        (vol.at[15], x_halo.at[0], (right, y)),
        (faces.at[0], y_halo.at[1], (x, down)),
        (faces.at[1], y_halo.at[0], (x, up)),
        (corners.at[0], c_halo.at[3], (left, down)),
        (corners.at[1], c_halo.at[2], (right, down)),
        (corners.at[2], c_halo.at[1], (left, up)),
        (corners.at[3], c_halo.at[0], (right, up)),
    ]
    barrier = pltpu.get_barrier_semaphore()
    for _, _, device in plan:
        pl.semaphore_signal(barrier, inc=1, device_id=device, device_id_type=MESH)
    pl.semaphore_wait(barrier, len(plan))
    copies = []
    for number, (source, target, device) in enumerate(plan):
        copy = pltpu.make_async_remote_copy(
            src_ref=source,
            dst_ref=target,
            send_sem=send_sem.at[number],
            recv_sem=recv_sem.at[number],
            device_id=device,
            device_id_type=MESH,
        )
        copy.start()
        copies.append(copy)
    for copy in copies:
        copy.wait()


def halo_exchange(vol, faces, corners, number):
    return pl.pallas_call(
        halo_kernel,
        out_shape=(jax.ShapeDtypeStruct((2, 2, 8, LINE), BF16), FACES, CORNERS),
        in_specs=[ANY] * 3,
        out_specs=(ANY,) * 3,
        scratch_shapes=[pltpu.SemaphoreType.DMA((8,)), pltpu.SemaphoreType.DMA((8,))],
        compiler_params=pltpu.CompilerParams(collective_id=number, has_side_effects=True),
        name="halo",
    )(vol, faces, corners)


def load_volume(info, own, x_halo, y_halo, c_halo, wide, sems):
    inner = pl.ds(C, LINE)
    copies = [
        pltpu.make_async_copy(own, wide.at[pl.ds(1, 16), pl.ds(1, 2), :, inner], sems.at[0]),
        pltpu.make_async_copy(x_halo.at[0], wide.at[0, pl.ds(1, 2), :, inner], sems.at[1]),
        pltpu.make_async_copy(x_halo.at[1], wide.at[17, pl.ds(1, 2), :, inner], sems.at[2]),
    ]
    for copy in copies:
        copy.start()
    margin = jnp.zeros((18, 4, 8, C), BF16)
    wide[:, :, :, 0:C] = margin
    wide[:, :, :, C + LINE : WIDE] = margin
    for side in range(2):
        block = 3 * side
        inside_y = info[34 + side] > 0
        for half in range(2):
            face = jnp.where(inside_y, y_halo[side, half].astype(F32), 0.0)
            for row in range(8):
                wide[1 + 8 * half + row, block, :, inner] = jnp.broadcast_to(
                    face[row : row + 1], (8, LINE)
                ).astype(BF16)
        for end in range(2):
            inside = inside_y & (info[32 + end] > 0)
            corner = jnp.where(inside, c_halo[2 * side + end].astype(F32), 0.0)
            for z in range(8):
                wide[17 * end, block, :, pl.ds(C + z * BRICK, BRICK)] = jnp.broadcast_to(
                    corner[z : z + 1], (8, BRICK)
                ).astype(BF16)
    for copy in copies:
        copy.wait()
    for end in range(2):

        @pl.when(info[32 + end] == 0)
        def _():
            wide[17 * end, 1:3, :, inner] = jnp.zeros((2, 8, LINE), BF16)


def cut_patch(wide, spot, even, odd):
    xb, yb, zb = spot
    lanes = pl.ds(pl.multiple_of(zb * BRICK, C), PATCH)
    rows = pl.ds(xb * 8, 10)
    before = wide[rows, yb, :, lanes].astype(F32)
    here = wide[rows, yb + 1, :, lanes].astype(F32)
    after = wide[rows, yb + 2, :, lanes].astype(F32)
    line = lax.broadcasted_iota(jnp.int32, here.shape, 1)
    shifts = [
        pltpu.roll(jnp.where(line == 7, before, here), 1, 1),
        here,
        pltpu.roll(jnp.where(line == 0, after, here), 7, 1),
    ]
    for b in range(3):
        even[b] = shifts[b].reshape(80, PATCH).astype(BF16)
        odd[b] = shifts[b][1:9].reshape(64, PATCH).astype(BF16)


def window(even, odd, a, b):
    parts = []
    for g in range(GROUP):
        for j in range(4):
            lanes = pl.ds(2 * C * j, 4 * C)
            parts.append(odd[g, b, :, lanes] if a == 1 else even[g, b, pl.ds(8 * a, 64), lanes])
    return jnp.concatenate(parts, axis=0)


def fill_band(band, taps):
    depth = taps.shape[1]
    band[...] = jnp.zeros(band.shape, BF16)
    for tap in range(9):
        for c in range(3):
            for o in range(2):
                band[tap, pl.ds((c + o) * C, depth), pl.ds(o * C, C)] = taps[3 * tap + c]


def convolve(even, odd, band):
    total = jnp.zeros((GROUP * 256, 2 * C), F32)
    for a in range(3):
        for b in range(3):
            total = total + jnp.dot(
                window(even, odd, a, b), band[3 * a + b], preferred_element_type=F32
            )
    return total


def add_taps(sums, slopes, even, odd):
    turned = slopes.astype(F32).T.astype(BF16)
    for a in range(3):
        for b in range(3):
            sums[3 * a + b] += jnp.dot(
                turned, window(even, odd, a, b), preferred_element_type=F32
            )


def gather_taps(sums, grad, depth):
    for tap in range(9):
        for c in range(3):
            part = (
                sums[tap, 0:C, c * C : (c + 1) * C]
                + sums[tap, C : 2 * C, (c + 1) * C : (c + 2) * C]
            )
            grad[pl.ds((3 * tap + c) * depth, depth)] = part.T[0:depth].astype(BF16)


def groups(info, order, act):
    def step(number, _):
        members = []
        for g in range(GROUP):
            position = number * GROUP + g
            place = order[position]
            slot = info[place]
            members.append((position, place, jnp.maximum(slot, 0), slot >= 0))
        act(number, members)
        return 0

    lax.fori_loop(0, (order[32] + GROUP - 1) // GROUP, step, 0)


def spread_mask(keep):
    blocks = []
    for j in range(4):
        pair = [jnp.broadcast_to(keep[:, 2 * j + o : 2 * j + o + 1], (64, C)) for o in range(2)]
        blocks.append(jnp.concatenate(pair, axis=1))
    return jnp.concatenate(blocks, axis=0)


def sigmoid(value):
    return 1.0 / (1.0 + jnp.exp(-value))


def first_kernel(
    info, order, own, x_halo, y_halo, c_halo, mask, taps, bias,
    vol, faces, corners, gates,
    wide, band, even, odd, sems,
):
    load_volume(info, own, x_halo, y_halo, c_halo, wide, sems)
    fill_band(band, taps)
    vol[...] = jnp.zeros(vol.shape, BF16)
    faces[...] = jnp.zeros(faces.shape, BF16)

    def forward(number, members):
        for g, (_, place, _, _) in enumerate(members):
            cut_patch(wide, coords(place), even.at[g], odd.at[g])
        both = convolve(even, odd, band) + bias[...]
        for g, (position, place, slot, live) in enumerate(members):
            linear = both[256 * g : 256 * g + 256]
            keep = jnp.where(live, spread_mask(mask[slot]), 0.0)
            sig = sigmoid(linear)
            hidden = keep * (linear * sig)
            gates[position] = (keep * (sig * (1.0 + linear * (1.0 - sig)))).astype(BF16)
            for j in range(4):
                piece = hidden[64 * j : 64 * j + 64].reshape(8, 8, 2 * C)
                put(vol, faces, coords(place), 2 * C * j, piece)

    groups(info, order, forward)
    put_corners(faces, corners)


def second_kernel(
    info, order, own, x_halo, y_halo, c_halo, mask, taps, bias, cots,
    vol, faces, corners, results, grad,
    wide, band, even, odd, sums, slopes, sems,
):
    load_volume(info, own, x_halo, y_halo, c_halo, wide, sems)
    fill_band(band, taps)
    vol[...] = jnp.zeros(vol.shape, BF16)
    faces[...] = jnp.zeros(faces.shape, BF16)
    sums[...] = jnp.zeros(sums.shape, F32)

    def forward(number, members):
        for g, (_, place, _, _) in enumerate(members):
            cut_patch(wide, coords(place), even.at[g], odd.at[g])
        both = convolve(even, odd, band) + bias[...]
        for g, (position, place, slot, live) in enumerate(members):
            worker = info[36 + slot]
            linear = both[256 * g : 256 * g + 256]
            keep = jnp.where(live, spread_mask(mask[slot]), 0.0)
            sig = sigmoid(linear)
            output = keep * (linear * sig)
            slope = keep * (sig * (1.0 + linear * (1.0 - sig)))
            for j in range(4):
                rows = slice(64 * j, 64 * j + 64)
                lanes = pl.ds(2 * C * j, 2 * C)
                piece = cots[worker, :, :, lanes].astype(F32).reshape(64, 2 * C) * slope[rows]
                slopes[position, pl.ds(64 * j, 64)] = piece.astype(BF16)
                put(vol, faces, coords(place), 2 * C * j, piece.reshape(8, 8, 2 * C))

            @pl.when(live)
            def _():
                for j in range(4):
                    rows = output[64 * j : 64 * j + 64].reshape(8, 8, 2 * C)
                    results[worker, :, :, pl.ds(2 * C * j, 2 * C)] = rows.astype(BF16)

    def backward(number, members):
        for g, (_, place, _, _) in enumerate(members):
            cut_patch(wide, coords(place), even.at[g], odd.at[g])
        rows = slopes[pl.ds(number * GROUP, GROUP)].reshape(GROUP * 256, 2 * C)
        add_taps(sums, rows, even, odd)

    groups(info, order, forward)
    put_corners(faces, corners)
    groups(info, order, backward)
    gather_taps(sums, grad, C)


def third_kernel(
    info, order, own, x_halo, y_halo, c_halo, own_in, x_halo_in, y_halo_in, c_halo_in, gates,
    taps, grad_two, c_in,
    grads,
    wide, wide_in, band, even, odd, sums, slopes, sems, sems_in,
):
    load_volume(info, own_in, x_halo_in, y_halo_in, c_halo_in, wide_in, sems_in)
    load_volume(info, own, x_halo, y_halo, c_halo, wide, sems)
    fill_band(band, taps)
    sums[...] = jnp.zeros(sums.shape, F32)

    def back(number, members):
        for g, (_, place, _, _) in enumerate(members):
            cut_patch(wide, coords(place), even.at[g], odd.at[g])
        both = convolve(even, odd, band)
        for g, (position, _, _, _) in enumerate(members):
            rows = both[256 * g : 256 * g + 256] * gates[position].astype(F32)
            slopes[position] = rows.astype(BF16)

    def backward(number, members):
        for g, (_, place, _, _) in enumerate(members):
            cut_patch(wide_in, coords(place), even.at[g], odd.at[g])
        rows = slopes[pl.ds(number * GROUP, GROUP)].reshape(GROUP * 256, 2 * C)
        add_taps(sums, rows, even, odd)

    groups(info, order, back)
    groups(info, order, backward)
    gather_taps(sums, grads, c_in)
    first_rows, second_rows = 27 * c_in, grad_two.shape[0]
    grads[first_rows : first_rows + second_rows] = grad_two[...]
    rest = grads.shape[0] - first_rows - second_rows
    grads[first_rows + second_rows :] = jnp.zeros((rest, C), BF16)


def reduce_kernel(
    grads,
    final,
    from_core, half, parts, line, send_sem, recv_sem,
):
    nx, ny = lax.axis_size("gx"), lax.axis_size("gy")
    x, y = lax.axis_index("gx"), lax.axis_index("gy")
    core, chip = lax.rem(y, 2), y // 2
    partner = (x, y + 1 - 2 * core)
    across = [(lax.rem(x + k, nx), y) for k in range(1, nx)]
    along = [(x, 2 * lax.rem(chip + k, ny // 2) + core) for k in range(1, ny // 2)]
    count = half.shape[0]
    chunk = count // nx
    mine = pl.multiple_of(core * count, count)
    others = pl.multiple_of((1 - core) * count, count)
    kept = pl.ds(pl.multiple_of(mine + x * chunk, chunk), chunk)

    barrier = pltpu.get_barrier_semaphore()
    peers = [partner] + across + along
    for device in peers:
        pl.semaphore_signal(barrier, inc=1, device_id=device, device_id_type=MESH)
    pl.semaphore_wait(barrier, len(peers))

    def send(source, target, device, number):
        copy = pltpu.make_async_remote_copy(
            src_ref=source,
            dst_ref=target,
            send_sem=send_sem.at[number],
            recv_sem=recv_sem.at[number],
            device_id=device,
            device_id_type=MESH,
        )
        copy.start()
        return copy

    send(grads.at[pl.ds(others, count)], from_core, partner, 0).wait()
    half[...] = (grads[pl.ds(mine, count)].astype(F32) + from_core[...].astype(F32)).astype(BF16)

    copies = []
    for k, device in enumerate(across):
        rows = pl.ds(pl.multiple_of(device[0] * chunk, chunk), chunk)
        copies.append(send(half.at[rows], parts.at[k], device, 1 + k))
    total = half[pl.ds(pl.multiple_of(x * chunk, chunk), chunk)].astype(F32)
    for k, copy in enumerate(copies):
        copy.wait()
        total = total + parts[k].astype(F32)

    line[chip] = total.astype(BF16)
    copies = [send(line.at[chip], line.at[chip], d, nx + k) for k, d in enumerate(along)]
    for copy in copies:
        copy.wait()
    total = line[0].astype(F32)
    for k in range(1, ny // 2):
        total = total + line[k].astype(F32)
    final[kept] = total.astype(BF16)

    first = nx + len(along)
    copies = [send(final.at[kept], final.at[kept], d, first + k) for k, d in enumerate(across)]
    for copy in copies:
        copy.wait()
    part = final.at[pl.ds(mine, count)]
    send(part, part, partner, first + len(across)).wait()


def reduce_grads(grads, nx, ny):
    count = grads.shape[0] // 2
    sems = 2 * nx + ny // 2 - 1
    return pl.pallas_call(
        reduce_kernel,
        out_shape=jax.ShapeDtypeStruct(grads.shape, BF16),
        in_specs=[VMEM],
        out_specs=VMEM,
        scratch_shapes=[
            pltpu.VMEM((count, C), BF16),
            pltpu.VMEM((count, C), BF16),
            pltpu.VMEM((nx - 1, count // nx, C), BF16),
            pltpu.VMEM((ny // 2, count // nx, C), BF16),
            pltpu.SemaphoreType.DMA((sems,)),
            pltpu.SemaphoreType.DMA((sems,)),
        ],
        compiler_params=pltpu.CompilerParams(
            collective_id=3, has_side_effects=True, vmem_limit_bytes=LIMIT
        ),
        name="reduce",
    )(grads)


def finish_kernel(sender, grads, arrived, result, grad_one, grad_two):
    for number in range(result.shape[0]):
        result[number] = arrived[sender[number]]
    first = 0
    for out in (grad_one, grad_two):
        rows = grads[first : first + out.shape[0]].astype(F32)
        out[...] = rows * lax.rsqrt(jnp.mean(rows * rows) + 1e-05)
        first += out.shape[0]


WIDE_SCRATCH = pltpu.VMEM((18, 4, 8, WIDE), BF16)
BAND_SCRATCH = pltpu.VMEM((9, 4 * C, 2 * C), BF16)
EVEN_SCRATCH = pltpu.VMEM((GROUP, 3, 80, PATCH), BF16)
ODD_SCRATCH = pltpu.VMEM((GROUP, 3, 64, PATCH), BF16)
SLOPES_SCRATCH = pltpu.VMEM((16, 256, 2 * C), BF16)
SUMS_SCRATCH = pltpu.VMEM((9, 2 * C, 4 * C), F32)
SEMS = pltpu.SemaphoreType.DMA((3,))
PARAMS = pltpu.CompilerParams(vmem_limit_bytes=LIMIT)


def body(
    features,
    voxel_mask,
    occupancy,
    send_counts,
    weight_one,
    bias_one,
    weight_two,
    bias_two,
    cotangent,
):
    x, y = lax.axis_index("gx"), lax.axis_index("gy")
    nx, ny = lax.axis_size("gx"), lax.axis_size("gy")
    c_in = weight_one.shape[1]
    lanes = jnp.arange(16, dtype=jnp.int32)
    table = send_counts[0]
    outgoing = table[x]
    incoming = table[:, x]
    start = jnp.cumsum(outgoing) - outgoing
    rank = jnp.cumsum(incoming) - incoming
    hits = (start[None, :] == lanes[:, None]) & (outgoing[None, :] > 0)
    worker = jnp.sum(jnp.where(hits, lanes[None, :], 0), axis=1)
    edges = jnp.stack([x > 0, x < nx - 1, y > 0, y < ny - 1]).astype(jnp.int32)
    info = jnp.concatenate([occupancy.reshape(32), edges, worker.astype(jnp.int32)])

    cots = lax.all_to_all(
        cotangent[0, 0][jnp.minimum(rank, 7)], "gx", split_axis=0, concat_axis=0, tiled=True
    )
    mask = voxel_mask[0, 0].reshape(16, 64, 8).astype(F32)
    *vol_in, order = pl.pallas_call(
        volume_kernel,
        out_shape=(VOLUME, FACES, CORNERS, jax.ShapeDtypeStruct((33,), jnp.int32)),
        in_specs=[SMEM, VMEM, VMEM],
        out_specs=(VMEM, VMEM, VMEM, SMEM),
        compiler_params=PARAMS,
        name="volume",
    )(info, features[0, 0], mask)
    halo_in = halo_exchange(*vol_in, 0)

    *hidden, gates = pl.pallas_call(
        first_kernel,
        out_shape=(VOLUME, FACES, CORNERS, jax.ShapeDtypeStruct((16, 256, 2 * C), BF16)),
        in_specs=[SMEM, SMEM, ANY, ANY, VMEM, VMEM, VMEM, VMEM, VMEM],
        out_specs=(VMEM,) * 4,
        scratch_shapes=[WIDE_SCRATCH, BAND_SCRATCH, EVEN_SCRATCH, ODD_SCRATCH, SEMS],
        compiler_params=PARAMS,
        name="first",
    )(info, order, vol_in[0], *halo_in, mask, weight_one, jnp.tile(bias_one, 2)[None])
    halo_mid = halo_exchange(*hidden, 1)

    *slopes, results, grad_two = pl.pallas_call(
        second_kernel,
        out_shape=(
            VOLUME,
            FACES,
            CORNERS,
            jax.ShapeDtypeStruct((16, 8, 8, BRICK), BF16),
            jax.ShapeDtypeStruct((27 * C, C), BF16),
        ),
        in_specs=[SMEM, SMEM, ANY, ANY, VMEM, VMEM, VMEM, VMEM, VMEM, VMEM],
        out_specs=(VMEM,) * 5,
        scratch_shapes=[
            WIDE_SCRATCH, BAND_SCRATCH, EVEN_SCRATCH, ODD_SCRATCH, SUMS_SCRATCH,
            SLOPES_SCRATCH, SEMS,
        ],
        compiler_params=PARAMS,
        name="second",
    )(info, order, hidden[0], *halo_mid, mask, weight_two, jnp.tile(bias_two, 2)[None], cots)
    halo_back = halo_exchange(*slopes, 2)
    halo_back, results = lax.optimization_barrier((halo_back, results))
    arrived = lax.all_to_all(results, "gx", split_axis=0, concat_axis=0, tiled=True)

    mirrored = weight_two[::-1].transpose(0, 2, 1)
    blocks = (27 * (c_in + C) // 16 + nx * ny - 1) // (nx * ny)
    grads = pl.pallas_call(
        lambda *refs: third_kernel(*refs[:13], c_in, *refs[13:]),
        out_shape=jax.ShapeDtypeStruct((16 * nx * ny * blocks, C), BF16),
        in_specs=[SMEM, SMEM, ANY, ANY, VMEM, VMEM, ANY, ANY, VMEM, VMEM, VMEM, VMEM, VMEM],
        out_specs=VMEM,
        scratch_shapes=[
            WIDE_SCRATCH, WIDE_SCRATCH, BAND_SCRATCH, EVEN_SCRATCH, ODD_SCRATCH, SUMS_SCRATCH,
            SLOPES_SCRATCH, SEMS, SEMS,
        ],
        compiler_params=PARAMS,
        cost_estimate=pl.CostEstimate(flops=33 * 10**9, bytes_accessed=10**8, transcendentals=0),
        name="third",
    )(info, order, slopes[0], *halo_back, vol_in[0], *halo_in, gates, mirrored, grad_two)
    grads = reduce_grads(grads, nx, ny)

    wanted = jnp.arange(8, dtype=jnp.int32)
    from_whom = (rank[None, :] == wanted[:, None]) & (incoming[None, :] > 0)
    sender = jnp.sum(jnp.where(from_whom, lanes[None, :], 0), axis=1)
    result, grad_one, grad_two = pl.pallas_call(
        finish_kernel,
        out_shape=(
            jax.ShapeDtypeStruct((8, 8, 8, BRICK), BF16),
            jax.ShapeDtypeStruct((27 * c_in, C), F32),
            jax.ShapeDtypeStruct((27 * C, C), F32),
        ),
        in_specs=[SMEM, VMEM, VMEM],
        out_specs=(VMEM,) * 3,
        compiler_params=PARAMS,
        name="finish",
    )(sender, grads, arrived)
    return (
        result[None, None],
        grad_one.reshape(weight_one.shape),
        grad_two.reshape(weight_two.shape),
    )


def solution(mesh):
    placed = (
        P("gx", "gy", None, None, None, None),
        P("gx", "gy", None, None),
        P("gx", "gy", None),
        P("gy", None, None),
        P(),
        P(),
        P(),
        P(),
        P("gx", "gy", None, None, None, None),
    )
    return jax.shard_map(
        body,
        mesh=mesh,
        in_specs=placed,
        out_specs=(P("gx", "gy", None, None, None, None), P(), P()),
        check_vma=False,
    )
```

```python
import functools

import jax
import jax.numpy as jnp
from jax import lax
from jax.experimental import pallas as pl
from jax.experimental.pallas import tpu as pltpu
from jax.sharding import PartitionSpec as P

MESH = pl.DeviceIdType.MESH
F32 = jnp.float32
BF16 = jnp.bfloat16
GROUP = 2
C = 128
BRICK = 8 * C
LINE = 8 * BRICK
WIDE = LINE + 2 * C
PATCH = BRICK + 2 * C
LIMIT = 60 * 1024 * 1024

VMEM = pl.BlockSpec(memory_space=pltpu.VMEM)
SMEM = pl.BlockSpec(memory_space=pltpu.SMEM)
ANY = pl.BlockSpec(memory_space=pl.ANY)

VOLUME = jax.ShapeDtypeStruct((16, 2, 8, LINE), BF16)
FACES = jax.ShapeDtypeStruct((2, 2, 8, LINE), BF16)
CORNERS = jax.ShapeDtypeStruct((4, 8, BRICK), BF16)


def coords(place):
    return place // 16, lax.rem(place // 8, 2), lax.rem(place, 8)


def put(vol, faces, spot, lane, value):
    xb, yb, zb = spot
    lanes = pl.ds(pl.multiple_of(zb * BRICK + lane, C), value.shape[2])
    vol[pl.ds(xb * 8, 8), yb, :, lanes] = value.astype(BF16)
    row = jnp.where(yb == 0, value[:, 0, :], value[:, 7, :])
    faces[yb, xb, :, lanes] = row.astype(BF16)


def put_corners(faces, corners):
    for side_y in range(2):
        for side_x in range(2):
            face = faces[side_y, side_x].astype(F32)
            row = face[7 * side_x : 7 * side_x + 1]
            rows = [row[:, z * BRICK : (z + 1) * BRICK] for z in range(8)]
            corners[2 * side_y + side_x] = jnp.concatenate(rows, axis=0).astype(BF16)


def volume_kernel(
    occupancy, counts, feat, mask, cotangent,
    vol, faces, corners, cots, info, order, sender,
):
    x, y = lax.axis_index("gx"), lax.axis_index("gy")
    info[32] = (x > 0).astype(jnp.int32)
    info[33] = (x < lax.axis_size("gx") - 1).astype(jnp.int32)
    info[34] = (y > 0).astype(jnp.int32)
    info[35] = (y < lax.axis_size("gy") - 1).astype(jnp.int32)

    def sort(place, numbers):
        active, empty = numbers
        xb, yb, zb = coords(place)
        slot = occupancy[xb, yb, zb]
        info[place] = slot
        live = slot >= 0
        order[jnp.where(live, active, 31 - empty)] = place
        one = live.astype(jnp.int32)
        return active + one, empty + 1 - one

    order[32] = lax.fori_loop(0, 32, sort, (0, 0))[0]

    def route(peer, numbers):
        slot, brick = numbers
        info[36 + slot] = peer
        sender[brick] = peer
        cots[peer] = cotangent[jnp.minimum(brick, 7)]
        return slot + counts[0, x, peer], brick + counts[0, peer, x]

    lax.fori_loop(0, 16, route, (0, 0))
    vol[...] = jnp.zeros(vol.shape, BF16)
    faces[...] = jnp.zeros(faces.shape, BF16)
    c_in = feat.shape[3] // 8

    def step(place, _):
        slot = info[place]

        @pl.when(slot >= 0)
        def _():
            rows = feat[slot].astype(F32)
            keep = mask[slot].reshape(8, 8, 8)
            pieces = []
            for w in range(8):
                pieces.append(rows[:, :, w * c_in : (w + 1) * c_in] * keep[:, :, w : w + 1])
                pieces.append(jnp.zeros((8, 8, C - c_in), F32))
            put(vol, faces, coords(place), 0, jnp.concatenate(pieces, axis=2))

        return 0

    lax.fori_loop(0, 32, step, 0)
    put_corners(faces, corners)


def halo_kernel(vol, faces, corners, x_halo, y_halo, c_halo, send_sem, recv_sem):
    nx, ny = lax.axis_size("gx"), lax.axis_size("gy")
    x, y = lax.axis_index("gx"), lax.axis_index("gy")
    left, right = lax.rem(x + nx - 1, nx), lax.rem(x + 1, nx)
    down, up = lax.rem(y + ny - 1, ny), lax.rem(y + 1, ny)
    plan = [
        (vol.at[0], x_halo.at[1], (left, y)),
        (vol.at[15], x_halo.at[0], (right, y)),
        (faces.at[0], y_halo.at[1], (x, down)),
        (faces.at[1], y_halo.at[0], (x, up)),
        (corners.at[0], c_halo.at[3], (left, down)),
        (corners.at[1], c_halo.at[2], (right, down)),
        (corners.at[2], c_halo.at[1], (left, up)),
        (corners.at[3], c_halo.at[0], (right, up)),
    ]
    barrier = pltpu.get_barrier_semaphore()
    for _, _, device in plan:
        pl.semaphore_signal(barrier, inc=1, device_id=device, device_id_type=MESH)
    pl.semaphore_wait(barrier, len(plan))
    copies = []
    for number, (source, target, device) in enumerate(plan):
        copy = pltpu.make_async_remote_copy(
            src_ref=source,
            dst_ref=target,
            send_sem=send_sem.at[number],
            recv_sem=recv_sem.at[number],
            device_id=device,
            device_id_type=MESH,
        )
        copy.start()
        copies.append(copy)
    for copy in copies:
        copy.wait()


def halo_exchange(vol, faces, corners, number):
    return pl.pallas_call(
        halo_kernel,
        out_shape=(jax.ShapeDtypeStruct((2, 2, 8, LINE), BF16), FACES, CORNERS),
        in_specs=[ANY] * 3,
        out_specs=(ANY,) * 3,
        scratch_shapes=[pltpu.SemaphoreType.DMA((8,)), pltpu.SemaphoreType.DMA((8,))],
        compiler_params=pltpu.CompilerParams(collective_id=number, has_side_effects=True),
        name="halo",
    )(vol, faces, corners)


def load_volume(info, own, x_halo, y_halo, c_halo, wide, sems):
    inner = pl.ds(C, LINE)
    copies = [
        pltpu.make_async_copy(own, wide.at[pl.ds(1, 16), pl.ds(1, 2), :, inner], sems.at[0]),
        pltpu.make_async_copy(x_halo.at[0], wide.at[0, pl.ds(1, 2), :, inner], sems.at[1]),
        pltpu.make_async_copy(x_halo.at[1], wide.at[17, pl.ds(1, 2), :, inner], sems.at[2]),
    ]
    for copy in copies:
        copy.start()
    margin = jnp.zeros((18, 4, 8, C), BF16)
    wide[:, :, :, 0:C] = margin
    wide[:, :, :, C + LINE : WIDE] = margin
    for side in range(2):
        block = 3 * side
        inside_y = info[34 + side] > 0
        for half in range(2):
            face = jnp.where(inside_y, y_halo[side, half].astype(F32), 0.0)
            for row in range(8):
                wide[1 + 8 * half + row, block, :, inner] = jnp.broadcast_to(
                    face[row : row + 1], (8, LINE)
                ).astype(BF16)
        for end in range(2):
            inside = inside_y & (info[32 + end] > 0)
            corner = jnp.where(inside, c_halo[2 * side + end].astype(F32), 0.0)
            for z in range(8):
                wide[17 * end, block, :, pl.ds(C + z * BRICK, BRICK)] = jnp.broadcast_to(
                    corner[z : z + 1], (8, BRICK)
                ).astype(BF16)
    for copy in copies:
        copy.wait()
    for end in range(2):

        @pl.when(info[32 + end] == 0)
        def _():
            wide[17 * end, 1:3, :, inner] = jnp.zeros((2, 8, LINE), BF16)


def cut_patch(wide, spot, even, odd):
    xb, yb, zb = spot
    lanes = pl.ds(pl.multiple_of(zb * BRICK, C), PATCH)
    rows = pl.ds(xb * 8, 10)
    before = wide[rows, yb, :, lanes].astype(F32)
    here = wide[rows, yb + 1, :, lanes].astype(F32)
    after = wide[rows, yb + 2, :, lanes].astype(F32)
    line = lax.broadcasted_iota(jnp.int32, here.shape, 1)
    shifts = [
        pltpu.roll(jnp.where(line == 7, before, here), 1, 1),
        here,
        pltpu.roll(jnp.where(line == 0, after, here), 7, 1),
    ]
    for b in range(3):
        even[b] = shifts[b].reshape(80, PATCH).astype(BF16)
        odd[b] = shifts[b][1:9].reshape(64, PATCH).astype(BF16)


def window(even, odd, a, b):
    parts = []
    for g in range(GROUP):
        for j in range(4):
            lanes = pl.ds(2 * C * j, 4 * C)
            parts.append(odd[g, b, :, lanes] if a == 1 else even[g, b, pl.ds(8 * a, 64), lanes])
    return jnp.concatenate(parts, axis=0)


def fill_band(band, taps, mirrored=False):
    depth = taps.shape[1]
    band[...] = jnp.zeros(band.shape, BF16)
    for tap in range(9):
        for c in range(3):
            block = taps[26 - 3 * tap - c].T if mirrored else taps[3 * tap + c]
            for o in range(2):
                band[tap, pl.ds((c + o) * C, depth), pl.ds(o * C, C)] = block


def convolve(even, odd, band):
    total = jnp.zeros((GROUP * 256, 2 * C), F32)
    for a in range(3):
        for b in range(3):
            total = total + jnp.dot(
                window(even, odd, a, b), band[3 * a + b], preferred_element_type=F32
            )
    return total


def add_taps(sums, slopes, even, odd):
    turned = slopes.astype(F32).T.astype(BF16)
    for a in range(3):
        for b in range(3):
            sums[3 * a + b] += jnp.dot(
                turned, window(even, odd, a, b), preferred_element_type=F32
            )


def gather_taps(sums, grad, depth):
    for tap in range(9):
        for c in range(3):
            part = (
                sums[tap, 0:C, c * C : (c + 1) * C]
                + sums[tap, C : 2 * C, (c + 1) * C : (c + 2) * C]
            )
            grad[pl.ds((3 * tap + c) * depth, depth)] = part.T[0:depth].astype(BF16)


def groups(info, order, act):
    def step(number, _):
        members = []
        for g in range(GROUP):
            position = number * GROUP + g
            place = order[position]
            slot = info[place]
            members.append((position, place, jnp.maximum(slot, 0), slot >= 0))
        act(number, members)
        return 0

    lax.fori_loop(0, (order[32] + GROUP - 1) // GROUP, step, 0)


def spread_mask(keep):
    blocks = []
    for j in range(4):
        pair = [jnp.broadcast_to(keep[:, 2 * j + o : 2 * j + o + 1], (64, C)) for o in range(2)]
        blocks.append(jnp.concatenate(pair, axis=1))
    return jnp.concatenate(blocks, axis=0)


def sigmoid(value):
    return 1.0 / (1.0 + jnp.exp(-value))


def first_kernel(
    info, order, own, x_halo, y_halo, c_halo, mask, taps, bias,
    vol, faces, corners, gates,
    wide, band, even, odd, sems,
):
    load_volume(info, own, x_halo, y_halo, c_halo, wide, sems)
    fill_band(band, taps)
    vol[...] = jnp.zeros(vol.shape, BF16)
    faces[...] = jnp.zeros(faces.shape, BF16)

    def forward(number, members):
        for g, (_, place, _, _) in enumerate(members):
            cut_patch(wide, coords(place), even.at[g], odd.at[g])
        both = convolve(even, odd, band) + bias[...]
        for g, (position, place, slot, live) in enumerate(members):
            linear = both[256 * g : 256 * g + 256]
            keep = jnp.where(live, spread_mask(mask[slot]), 0.0)
            sig = sigmoid(linear)
            hidden = keep * (linear * sig)
            gates[position] = (keep * (sig * (1.0 + linear * (1.0 - sig)))).astype(BF16)
            for j in range(4):
                piece = hidden[64 * j : 64 * j + 64].reshape(8, 8, 2 * C)
                put(vol, faces, coords(place), 2 * C * j, piece)

    groups(info, order, forward)
    put_corners(faces, corners)


def second_kernel(
    info, order, own, x_halo, y_halo, c_halo, mask, taps, bias, cots,
    vol, faces, corners, results, grad,
    wide, band, even, odd, sums, slopes, sems,
):
    load_volume(info, own, x_halo, y_halo, c_halo, wide, sems)
    fill_band(band, taps)
    vol[...] = jnp.zeros(vol.shape, BF16)
    faces[...] = jnp.zeros(faces.shape, BF16)
    sums[...] = jnp.zeros(sums.shape, F32)

    def forward(number, members):
        for g, (_, place, _, _) in enumerate(members):
            cut_patch(wide, coords(place), even.at[g], odd.at[g])
        both = convolve(even, odd, band) + bias[...]
        for g, (position, place, slot, live) in enumerate(members):
            worker = info[36 + slot]
            linear = both[256 * g : 256 * g + 256]
            keep = jnp.where(live, spread_mask(mask[slot]), 0.0)
            sig = sigmoid(linear)
            output = keep * (linear * sig)
            slope = keep * (sig * (1.0 + linear * (1.0 - sig)))
            for j in range(4):
                rows = slice(64 * j, 64 * j + 64)
                lanes = pl.ds(2 * C * j, 2 * C)
                piece = cots[worker, :, :, lanes].astype(F32).reshape(64, 2 * C) * slope[rows]
                slopes[position, pl.ds(64 * j, 64)] = piece.astype(BF16)
                put(vol, faces, coords(place), 2 * C * j, piece.reshape(8, 8, 2 * C))

            @pl.when(live)
            def _():
                for j in range(4):
                    rows = output[64 * j : 64 * j + 64].reshape(8, 8, 2 * C)
                    results[worker, :, :, pl.ds(2 * C * j, 2 * C)] = rows.astype(BF16)

    def backward(number, members):
        for g, (_, place, _, _) in enumerate(members):
            cut_patch(wide, coords(place), even.at[g], odd.at[g])
        rows = slopes[pl.ds(number * GROUP, GROUP)].reshape(GROUP * 256, 2 * C)
        add_taps(sums, rows, even, odd)

    groups(info, order, forward)
    put_corners(faces, corners)
    groups(info, order, backward)
    gather_taps(sums, grad, C)


def third_kernel(
    info, order, own, x_halo, y_halo, c_halo, own_in, x_halo_in, y_halo_in, c_halo_in, gates,
    taps, grad_two, c_in,
    grads,
    wide, wide_in, band, even, odd, sums, slopes, sems, sems_in,
):
    load_volume(info, own_in, x_halo_in, y_halo_in, c_halo_in, wide_in, sems_in)
    load_volume(info, own, x_halo, y_halo, c_halo, wide, sems)
    fill_band(band, taps, mirrored=True)
    sums[...] = jnp.zeros(sums.shape, F32)

    def back(number, members):
        for g, (_, place, _, _) in enumerate(members):
            cut_patch(wide, coords(place), even.at[g], odd.at[g])
        both = convolve(even, odd, band)
        for g, (position, _, _, _) in enumerate(members):
            rows = both[256 * g : 256 * g + 256] * gates[position].astype(F32)
            slopes[position] = rows.astype(BF16)

    def backward(number, members):
        for g, (_, place, _, _) in enumerate(members):
            cut_patch(wide_in, coords(place), even.at[g], odd.at[g])
        rows = slopes[pl.ds(number * GROUP, GROUP)].reshape(GROUP * 256, 2 * C)
        add_taps(sums, rows, even, odd)

    groups(info, order, back)
    groups(info, order, backward)
    gather_taps(sums, grads, c_in)
    first_rows, second_rows = 27 * c_in, grad_two.shape[0]
    grads[first_rows : first_rows + second_rows] = grad_two[...]
    rest = grads.shape[0] - first_rows - second_rows
    grads[first_rows + second_rows :] = jnp.zeros((rest, C), BF16)


def reduce_kernel(
    grads,
    final,
    from_core, half, got_1, sum_1, got_2, sum_2, got_3, send_sem, recv_sem,
):
    x, y = lax.axis_index("gx"), lax.axis_index("gy")
    core = lax.rem(y, 2)
    spot = {"x": x // 4, "z": lax.rem(x, 4), "y": y // 2}
    partner = (x, y + 1 - 2 * core)

    def peer(axis, k):
        at = lax.rem(spot[axis] + k, 4)
        if axis == "x":
            return at, (4 * at + spot["z"], y)
        if axis == "z":
            return at, (4 * spot["x"] + at, y)
        return at, (x, 2 * at + core)

    count = half.shape[0]
    part = count // 3
    size_1, size_2, size_3 = part // 4, part // 16, part // 64
    mine = pl.multiple_of(core * count, count)
    others = pl.multiple_of((1 - core) * count, count)
    axes = [("x", "z", "y"), ("z", "y", "x"), ("y", "x", "z")]
    steps = range(1, 4)

    barrier = pltpu.get_barrier_semaphore()
    everyone = [partner] + [peer(axis, k)[1] for axis in "xyz" for k in steps]
    for device in everyone:
        pl.semaphore_signal(barrier, inc=1, device_id=device, device_id_type=MESH)
    pl.semaphore_wait(barrier, len(everyone))

    used = iter(range(send_sem.shape[0]))

    def send(source, target, device):
        number = next(used)
        copy = pltpu.make_async_remote_copy(
            src_ref=source,
            dst_ref=target,
            send_sem=send_sem.at[number],
            recv_sem=recv_sem.at[number],
            device_id=device,
            device_id_type=MESH,
        )
        copy.start()
        return copy

    def finish(copies):
        for copy in copies:
            copy.wait()

    def rows(start, size):
        return pl.ds(pl.multiple_of(start, size), size)

    flights = [
        [send(grads.at[rows(others + p * part, part)], from_core.at[rows(p * part, part)], partner)]
        for p in range(3)
    ]
    for p in range(3):
        finish(flights[p])
        here = rows(p * part, part)
        kept = grads[rows(mine + p * part, part)].astype(F32)
        half[here] = (kept + from_core[here].astype(F32)).astype(BF16)
        flights[p] = []
        for k in steps:
            at, device = peer(axes[p][0], k)
            piece = half.at[rows(p * part + at * size_1, size_1)]
            flights[p].append(send(piece, got_1.at[3 * p + k - 1], device))
    for p in range(3):
        finish(flights[p])
        total = half[rows(p * part + spot[axes[p][0]] * size_1, size_1)].astype(F32)
        for k in steps:
            total = total + got_1[3 * p + k - 1].astype(F32)
        sum_1[p] = total
        flights[p] = []
        for k in steps:
            at, device = peer(axes[p][1], k)
            piece = sum_1.at[p, rows(at * size_2, size_2)]
            flights[p].append(send(piece, got_2.at[3 * p + k - 1], device))
    for p in range(3):
        finish(flights[p])
        total = sum_1[p, rows(spot[axes[p][1]] * size_2, size_2)]
        for k in steps:
            total = total + got_2[3 * p + k - 1]
        sum_2[p] = total
        flights[p] = []
        for k in steps:
            at, device = peer(axes[p][2], k)
            piece = sum_2.at[p, rows(at * size_3, size_3)]
            flights[p].append(send(piece, got_3.at[3 * p + k - 1], device))
    starts = []
    for p in range(3):
        start = mine + p * part + spot[axes[p][0]] * size_1
        middle = start + spot[axes[p][1]] * size_2
        starts.append((start, middle, middle + spot[axes[p][2]] * size_3))

    def spread(p, level, size):
        piece = final.at[rows(starts[p][level], size)]
        return [send(piece, piece, peer(axes[p][level], k)[1]) for k in steps]

    for p in range(3):
        finish(flights[p])
        total = sum_2[p, rows(spot[axes[p][2]] * size_3, size_3)]
        for k in steps:
            total = total + got_3[3 * p + k - 1]
        final[rows(starts[p][2], size_3)] = total.astype(BF16)
        flights[p] = spread(p, 2, size_3)
    for p in range(3):
        finish(flights[p])
        flights[p] = spread(p, 1, size_2)
    for p in range(3):
        finish(flights[p])
        flights[p] = spread(p, 0, size_1)
    for p in range(3):
        finish(flights[p])
        piece = final.at[rows(mine + p * part, part)]
        flights[p] = [send(piece, piece, partner)]
    for p in range(3):
        finish(flights[p])


def reduce_grads(grads):
    count = grads.shape[0] // 2
    part = count // 3
    return pl.pallas_call(
        reduce_kernel,
        out_shape=jax.ShapeDtypeStruct(grads.shape, BF16),
        in_specs=[VMEM],
        out_specs=VMEM,
        scratch_shapes=[
            pltpu.VMEM((count, C), BF16),
            pltpu.VMEM((count, C), BF16),
            pltpu.VMEM((9, part // 4, C), BF16),
            pltpu.VMEM((3, part // 4, C), F32),
            pltpu.VMEM((9, part // 16, C), F32),
            pltpu.VMEM((3, part // 16, C), F32),
            pltpu.VMEM((9, part // 64, C), F32),
            pltpu.SemaphoreType.DMA((60,)),
            pltpu.SemaphoreType.DMA((60,)),
        ],
        compiler_params=pltpu.CompilerParams(
            collective_id=3, has_side_effects=True, vmem_limit_bytes=LIMIT
        ),
        name="reduce",
    )(grads)


def finish_kernel(sender, grads, arrived, result, grad_one, grad_two):
    for number in range(result.shape[0]):
        result[number] = arrived[sender[number]]
    first = 0
    for out in (grad_one, grad_two):
        rows = grads[first : first + out.shape[0]].astype(F32)
        out[...] = rows * lax.rsqrt(jnp.mean(rows * rows) + 1e-05)
        first += out.shape[0]


WIDE_SCRATCH = pltpu.VMEM((18, 4, 8, WIDE), BF16)
BAND_SCRATCH = pltpu.VMEM((9, 4 * C, 2 * C), BF16)
EVEN_SCRATCH = pltpu.VMEM((GROUP, 3, 80, PATCH), BF16)
ODD_SCRATCH = pltpu.VMEM((GROUP, 3, 64, PATCH), BF16)
SLOPES_SCRATCH = pltpu.VMEM((16, 256, 2 * C), BF16)
SUMS_SCRATCH = pltpu.VMEM((9, 2 * C, 4 * C), F32)
SEMS = pltpu.SemaphoreType.DMA((3,))
PARAMS = pltpu.CompilerParams(vmem_limit_bytes=LIMIT)


def body(
    features,
    voxel_mask,
    occupancy,
    send_counts,
    weight_one,
    bias_one,
    weight_two,
    bias_two,
    cotangent,
):
    c_in = weight_one.shape[1]
    mask = voxel_mask[0, 0].reshape(16, 64, 8).astype(F32)
    *vol_in, cots, info, order, sender = pl.pallas_call(
        volume_kernel,
        out_shape=(
            VOLUME,
            FACES,
            CORNERS,
            jax.ShapeDtypeStruct((16, 8, 8, BRICK), BF16),
            jax.ShapeDtypeStruct((53,), jnp.int32),
            jax.ShapeDtypeStruct((33,), jnp.int32),
            jax.ShapeDtypeStruct((9,), jnp.int32),
        ),
        in_specs=[SMEM, SMEM, VMEM, VMEM, VMEM],
        out_specs=(VMEM,) * 4 + (SMEM,) * 3,
        compiler_params=PARAMS,
        name="volume",
    )(occupancy, send_counts, features[0, 0], mask, cotangent[0, 0])
    halo_in = halo_exchange(*vol_in, 0)
    halo_in, cots = lax.optimization_barrier((halo_in, cots))
    cots = lax.all_to_all(cots, "gx", split_axis=0, concat_axis=0, tiled=True)

    *hidden, gates = pl.pallas_call(
        first_kernel,
        out_shape=(VOLUME, FACES, CORNERS, jax.ShapeDtypeStruct((16, 256, 2 * C), BF16)),
        in_specs=[SMEM, SMEM, ANY, ANY, VMEM, VMEM, VMEM, VMEM, VMEM],
        out_specs=(VMEM,) * 4,
        scratch_shapes=[WIDE_SCRATCH, BAND_SCRATCH, EVEN_SCRATCH, ODD_SCRATCH, SEMS],
        compiler_params=PARAMS,
        cost_estimate=pl.CostEstimate(flops=11 * 10**9, bytes_accessed=10**8, transcendentals=0),
        name="first",
    )(info, order, vol_in[0], *halo_in, mask, weight_one, jnp.tile(bias_one, 2)[None])
    halo_mid = halo_exchange(*hidden, 1)

    *slopes, results, grad_two = pl.pallas_call(
        second_kernel,
        out_shape=(
            VOLUME,
            FACES,
            CORNERS,
            jax.ShapeDtypeStruct((16, 8, 8, BRICK), BF16),
            jax.ShapeDtypeStruct((27 * C, C), BF16),
        ),
        in_specs=[SMEM, SMEM, ANY, ANY, VMEM, VMEM, VMEM, VMEM, VMEM, VMEM],
        out_specs=(VMEM,) * 5,
        scratch_shapes=[
            WIDE_SCRATCH, BAND_SCRATCH, EVEN_SCRATCH, ODD_SCRATCH, SUMS_SCRATCH,
            SLOPES_SCRATCH, SEMS,
        ],
        compiler_params=PARAMS,
        name="second",
    )(info, order, hidden[0], *halo_mid, mask, weight_two, jnp.tile(bias_two, 2)[None], cots)
    halo_back = halo_exchange(*slopes, 2)
    halo_back, results = lax.optimization_barrier((halo_back, results))
    arrived = lax.all_to_all(results, "gx", split_axis=0, concat_axis=0, tiled=True)

    grads = pl.pallas_call(
        lambda *refs: third_kernel(*refs[:13], c_in, *refs[13:]),
        out_shape=jax.ShapeDtypeStruct((6144, C), BF16),
        in_specs=[SMEM, SMEM, ANY, ANY, VMEM, VMEM, ANY, ANY, VMEM, VMEM, VMEM, VMEM, VMEM],
        out_specs=VMEM,
        scratch_shapes=[
            WIDE_SCRATCH, WIDE_SCRATCH, BAND_SCRATCH, EVEN_SCRATCH, ODD_SCRATCH, SUMS_SCRATCH,
            SLOPES_SCRATCH, SEMS, SEMS,
        ],
        compiler_params=PARAMS,
        cost_estimate=pl.CostEstimate(flops=33 * 10**9, bytes_accessed=10**8, transcendentals=0),
        name="third",
    )(info, order, slopes[0], *halo_back, vol_in[0], *halo_in, gates, weight_two, grad_two)
    grads = reduce_grads(grads)

    result, grad_one, grad_two = pl.pallas_call(
        finish_kernel,
        out_shape=(
            jax.ShapeDtypeStruct((8, 8, 8, BRICK), BF16),
            jax.ShapeDtypeStruct((27 * c_in, C), F32),
            jax.ShapeDtypeStruct((27 * C, C), F32),
        ),
        in_specs=[SMEM, VMEM, VMEM],
        out_specs=(VMEM,) * 3,
        compiler_params=PARAMS,
        name="finish",
    )(sender, grads, arrived)
    return (
        result[None, None],
        grad_one.reshape(weight_one.shape),
        grad_two.reshape(weight_two.shape),
    )


def solution(mesh):
    placed = (
        P("gx", "gy", None, None, None, None),
        P("gx", "gy", None, None),
        P("gx", "gy", None),
        P("gy", None, None),
        P(),
        P(),
        P(),
        P(),
        P("gx", "gy", None, None, None, None),
    )
    return jax.shard_map(
        body,
        mesh=mesh,
        in_specs=placed,
        out_specs=(P("gx", "gy", None, None, None, None), P(), P()),
        check_vma=False,
    )
```

```python
import functools

import jax
import jax.numpy as jnp
from jax import lax
from jax.experimental import pallas as pl
from jax.experimental.pallas import tpu as pltpu
from jax.sharding import PartitionSpec as P

MESH = pl.DeviceIdType.MESH
F32 = jnp.float32
BF16 = jnp.bfloat16
GROUP = 2
C = 128
BRICK = 8 * C
LINE = 8 * BRICK
WIDE = LINE + 2 * C
PATCH = BRICK + 2 * C
LIMIT = 60 * 1024 * 1024

VMEM = pl.BlockSpec(memory_space=pltpu.VMEM)
SMEM = pl.BlockSpec(memory_space=pltpu.SMEM)
ANY = pl.BlockSpec(memory_space=pl.ANY)

VOLUME = jax.ShapeDtypeStruct((16, 2, 8, LINE), BF16)
FACES = jax.ShapeDtypeStruct((2, 2, 8, LINE), BF16)
CORNERS = jax.ShapeDtypeStruct((4, 8, BRICK), BF16)


def coords(place):
    return lax.div(place, 16), lax.rem(lax.div(place, 8), 2), lax.rem(place, 8)


def put(vol, faces, spot, lane, value):
    xb, yb, zb = spot
    lanes = pl.ds(pl.multiple_of(zb * BRICK + lane, C), value.shape[2])
    vol[pl.ds(xb * 8, 8), yb, :, lanes] = value.astype(BF16)
    row = jnp.where(yb == 0, value[:, 0, :], value[:, 7, :])
    faces[yb, xb, :, lanes] = row.astype(BF16)


def put_corners(faces, corners):
    for side_y in range(2):
        for side_x in range(2):
            face = faces[side_y, side_x].astype(F32)
            row = face[7 * side_x : 7 * side_x + 1]
            rows = [row[:, z * BRICK : (z + 1) * BRICK] for z in range(8)]
            corners[2 * side_y + side_x] = jnp.concatenate(rows, axis=0).astype(BF16)


def volume_kernel(
    occupancy, counts, feat, mask, cotangent,
    vol, faces, corners, cots, info, order, sender,
):
    x = lax.axis_index("gx")

    def sort(place, numbers):
        active, empty = numbers
        xb, yb, zb = coords(place)
        slot = occupancy[xb, yb, zb]
        info[place] = slot
        live = slot >= 0
        order[jnp.where(live, active, 31 - empty)] = place
        one = live.astype(jnp.int32)
        return active + one, empty + 1 - one

    order[32] = lax.fori_loop(0, 32, sort, (0, 0))[0]

    def route(peer, numbers):
        slot, brick = numbers
        info[32 + slot] = peer
        sender[brick] = peer
        cots[peer] = cotangent[jnp.minimum(brick, 7)]
        return slot + counts[0, x, peer], brick + counts[0, peer, x]

    lax.fori_loop(0, 16, route, (0, 0))
    vol[...] = jnp.zeros(vol.shape, BF16)
    faces[...] = jnp.zeros(faces.shape, BF16)
    c_in = feat.shape[3] // 8

    def step(place, _):
        slot = info[place]

        @pl.when(slot >= 0)
        def _():
            rows = feat[slot].astype(F32)
            keep = mask[slot].reshape(8, 8, 8)
            pieces = []
            for w in range(8):
                pieces.append(rows[:, :, w * c_in : (w + 1) * c_in] * keep[:, :, w : w + 1])
                pieces.append(jnp.zeros((8, 8, C - c_in), F32))
            put(vol, faces, coords(place), 0, jnp.concatenate(pieces, axis=2))

        return 0

    lax.fori_loop(0, 32, step, 0)
    put_corners(faces, corners)


def halo_plan(x_faces, faces, corners, x_halo, y_halo, c_halo):
    nx, ny = lax.axis_size("gx"), lax.axis_size("gy")
    x, y = lax.axis_index("gx"), lax.axis_index("gy")
    left, right = lax.rem(x + nx - 1, nx), lax.rem(x + 1, nx)
    down, up = lax.rem(y + ny - 1, ny), lax.rem(y + 1, ny)
    return [
        (x_faces[0], x_halo[1], (left, y)),
        (x_faces[1], x_halo[0], (right, y)),
        (faces.at[0], y_halo.at[1], (x, down)),
        (faces.at[1], y_halo.at[0], (x, up)),
        (corners.at[0], c_halo.at[3], (left, down)),
        (corners.at[1], c_halo.at[2], (right, down)),
        (corners.at[2], c_halo.at[1], (left, up)),
        (corners.at[3], c_halo.at[0], (right, up)),
    ]


def greet(devices):
    barrier = pltpu.get_barrier_semaphore()
    for device in devices:
        pl.semaphore_signal(barrier, inc=1, device_id=device, device_id_type=MESH)
    pl.semaphore_wait(barrier, len(devices))


def sender_of(send_sem, recv_sem):
    used = iter(range(send_sem.shape[0]))

    def send(source, target, device):
        number = next(used)
        copy = pltpu.make_async_remote_copy(
            src_ref=source,
            dst_ref=target,
            send_sem=send_sem.at[number],
            recv_sem=recv_sem.at[number],
            device_id=device,
            device_id_type=MESH,
        )
        copy.start()
        return copy

    return send


def finish(copies):
    for copy in copies:
        copy.wait()


def halo_kernel(vol, faces, corners, x_halo, y_halo, c_halo, send_sem, recv_sem):
    x_faces = (vol.at[0], vol.at[15])
    plan = halo_plan(x_faces, faces, corners, (x_halo.at[0], x_halo.at[1]), y_halo, c_halo)
    greet([device for _, _, device in plan])
    send = sender_of(send_sem, recv_sem)
    finish([send(*item) for item in plan])


def halo_exchange(vol, faces, corners, number):
    return pl.pallas_call(
        halo_kernel,
        out_shape=(jax.ShapeDtypeStruct((2, 2, 8, LINE), BF16), FACES, CORNERS),
        in_specs=[ANY] * 3,
        out_specs=(ANY,) * 3,
        scratch_shapes=[pltpu.SemaphoreType.DMA((8,)), pltpu.SemaphoreType.DMA((8,))],
        compiler_params=pltpu.CompilerParams(collective_id=number, has_side_effects=True),
        name="halo",
    )(vol, faces, corners)


def inside_slab():
    x, y = lax.axis_index("gx"), lax.axis_index("gy")
    nx, ny = lax.axis_size("gx"), lax.axis_size("gy")
    return (x > 0, x < nx - 1), (y > 0, y < ny - 1)


def open_volume(own, x_halo, wide, sems):
    inner = pl.ds(C, LINE)
    copies = [pltpu.make_async_copy(own, wide.at[pl.ds(1, 16), pl.ds(1, 2), :, inner], sems.at[0])]
    if x_halo is not None:
        for end in range(2):
            target = wide.at[17 * end, pl.ds(1, 2), :, inner]
            copies.append(pltpu.make_async_copy(x_halo.at[end], target, sems.at[1 + end]))
    for copy in copies:
        copy.start()
    return copies


def close_volume(y_halo, c_halo, wide, copies):
    inside_x, inside_y = inside_slab()
    inner = pl.ds(C, LINE)
    margin = jnp.zeros((18, 4, 8, C), BF16)
    wide[:, :, :, 0:C] = margin
    wide[:, :, :, C + LINE : WIDE] = margin
    for side in range(2):
        block = 3 * side
        for half in range(2):
            face = jnp.where(inside_y[side], y_halo[side, half].astype(F32), 0.0)
            for row in range(8):
                wide[1 + 8 * half + row, block, :, inner] = jnp.broadcast_to(
                    face[row : row + 1], (8, LINE)
                ).astype(BF16)
        for end in range(2):
            inside = inside_y[side] & inside_x[end]
            corner = jnp.where(inside, c_halo[2 * side + end].astype(F32), 0.0)
            for z in range(8):
                wide[17 * end, block, :, pl.ds(C + z * BRICK, BRICK)] = jnp.broadcast_to(
                    corner[z : z + 1], (8, BRICK)
                ).astype(BF16)
    finish(copies)
    for end in range(2):

        @pl.when(jnp.logical_not(inside_x[end]))
        def _():
            wide[17 * end, 1:3, :, inner] = jnp.zeros((2, 8, LINE), BF16)


def cut_patch(wide, spot, even, odd):
    xb, yb, zb = spot
    lanes = pl.ds(zb * BRICK, PATCH)
    rows = pl.ds(xb * 8, 10)
    before = wide[rows, yb, :, lanes].astype(F32)
    here = wide[rows, yb + 1, :, lanes].astype(F32)
    after = wide[rows, yb + 2, :, lanes].astype(F32)
    line = lax.broadcasted_iota(jnp.int32, here.shape, 1)
    shifts = [
        pltpu.roll(jnp.where(line == 7, before, here), 1, 1),
        here,
        pltpu.roll(jnp.where(line == 0, after, here), 7, 1),
    ]
    for b in range(3):
        even[b] = shifts[b].reshape(80, PATCH).astype(BF16)
        odd[b] = shifts[b][1:9].reshape(64, PATCH).astype(BF16)


def window(even, odd, a, b):
    parts = []
    for g in range(GROUP):
        for j in range(4):
            lanes = pl.ds(2 * C * j, 4 * C)
            parts.append(odd[g, b, :, lanes] if a == 1 else even[g, b, pl.ds(8 * a, 64), lanes])
    return jnp.concatenate(parts, axis=0)


def fill_band(band, taps, mirrored=False):
    depth = taps.shape[1]
    band[...] = jnp.zeros(band.shape, BF16)
    for tap in range(9):
        for c in range(3):
            block = taps[26 - 3 * tap - c].T if mirrored else taps[3 * tap + c]
            for o in range(2):
                band[tap, pl.ds((c + o) * C, depth), pl.ds(o * C, C)] = block


def convolve(even, odd, band):
    total = jnp.zeros((GROUP * 256, 2 * C), F32)
    for a in range(3):
        for b in range(3):
            total = total + jnp.dot(
                window(even, odd, a, b), band[3 * a + b], preferred_element_type=F32
            )
    return total


def add_taps(sums, slopes, even, odd):
    turned = slopes.astype(F32).T.astype(BF16)
    for a in range(3):
        for b in range(3):
            sums[3 * a + b] += jnp.dot(
                turned, window(even, odd, a, b), preferred_element_type=F32
            )


def gather_taps(sums, grad, depth, first):
    for tap in range(9):
        for c in range(3):
            part = (
                sums[tap, 0:C, c * C : (c + 1) * C]
                + sums[tap, C : 2 * C, (c + 1) * C : (c + 2) * C]
            )
            grad[pl.ds(first + (3 * tap + c) * depth, depth)] = part.T[0:depth].astype(BF16)


def groups(info, order, act, start, stop):
    def step(number, _):
        members = []
        for g in range(GROUP):
            position = number * GROUP + g
            place = order[position]
            slot = info[place]
            members.append((position, place, jnp.maximum(slot, 0), slot >= 0))
        act(number, members)
        return 0

    lax.fori_loop(start, stop, step, 0)


def all_groups(info, order, act):
    groups(info, order, act, 0, (order[32] + GROUP - 1) // GROUP)


def spread_mask(keep):
    blocks = []
    for j in range(4):
        pair = [jnp.broadcast_to(keep[:, 2 * j + o : 2 * j + o + 1], (64, C)) for o in range(2)]
        blocks.append(jnp.concatenate(pair, axis=1))
    return jnp.concatenate(blocks, axis=0)


def sigmoid(value):
    return 1.0 / (1.0 + jnp.exp(-value))


def first_kernel(
    info, order, own, x_halo, y_halo, c_halo, mask, taps, bias,
    vol, faces, corners, gates,
    wide, band, even, odd, sems,
):
    copies = open_volume(own, x_halo, wide, sems)
    fill_band(band, taps)
    vol[...] = jnp.zeros(vol.shape, BF16)
    faces[...] = jnp.zeros(faces.shape, BF16)

    def forward(number, members):
        for g, (_, place, _, _) in enumerate(members):
            cut_patch(wide, coords(place), even.at[g], odd.at[g])
        both = convolve(even, odd, band) + bias[...]
        for g, (position, place, slot, live) in enumerate(members):
            linear = both[256 * g : 256 * g + 256]
            keep = jnp.where(live, spread_mask(mask[slot]), 0.0)
            sig = sigmoid(linear)
            hidden = keep * (linear * sig)
            gates[position] = (keep * (sig * (1.0 + linear * (1.0 - sig)))).astype(BF16)
            for j in range(4):
                piece = hidden[64 * j : 64 * j + 64].reshape(8, 8, 2 * C)
                put(vol, faces, coords(place), 2 * C * j, piece)

    close_volume(y_halo, c_halo, wide, copies)
    all_groups(info, order, forward)
    put_corners(faces, corners)


def second_kernel(
    info, order, own, x_halo, y_halo, c_halo, mask, taps, bias, cots,
    vol, faces, corners, results, slopes,
    wide, band, even, odd, sems,
):
    copies = open_volume(own, x_halo, wide, sems)
    fill_band(band, taps)
    vol[...] = jnp.zeros(vol.shape, BF16)
    faces[...] = jnp.zeros(faces.shape, BF16)
    slopes[...] = jnp.zeros(slopes.shape, BF16)

    def forward(number, members):
        for g, (_, place, _, _) in enumerate(members):
            cut_patch(wide, coords(place), even.at[g], odd.at[g])
        both = convolve(even, odd, band) + bias[...]
        for g, (position, place, slot, live) in enumerate(members):
            worker = info[32 + slot]
            linear = both[256 * g : 256 * g + 256]
            keep = jnp.where(live, spread_mask(mask[slot]), 0.0)
            sig = sigmoid(linear)
            output = keep * (linear * sig)
            slope = keep * (sig * (1.0 + linear * (1.0 - sig)))
            for j in range(4):
                rows = slice(64 * j, 64 * j + 64)
                lanes = pl.ds(2 * C * j, 2 * C)
                piece = cots[worker, :, :, lanes].astype(F32).reshape(64, 2 * C) * slope[rows]
                slopes[position, pl.ds(64 * j, 64)] = piece.astype(BF16)
                put(vol, faces, coords(place), 2 * C * j, piece.reshape(8, 8, 2 * C))

            @pl.when(live)
            def _():
                for j in range(4):
                    rows = output[64 * j : 64 * j + 64].reshape(8, 8, 2 * C)
                    results[worker, :, :, pl.ds(2 * C * j, 2 * C)] = rows.astype(BF16)

    close_volume(y_halo, c_halo, wide, copies)
    all_groups(info, order, forward)
    put_corners(faces, corners)


def total_of(grads, final, base, parts, send, buffers):
    x, y = lax.axis_index("gx"), lax.axis_index("gy")
    core = lax.rem(y, 2)
    spot = {"x": x // 4, "z": lax.rem(x, 4), "y": y // 2}
    partner = (x, y + 1 - 2 * core)
    steps = range(1, 4)
    from_core, half, *part_buffers = buffers
    count = half.shape[0]
    mine, others = base + core * count, base + (1 - core) * count

    def peer(axis, k):
        at = lax.rem(spot[axis] + k, 4)
        if axis == "x":
            return at, (4 * at + spot["z"], y)
        if axis == "z":
            return at, (4 * spot["x"] + at, y)
        return at, (x, 2 * at + core)

    def rows(start, size):
        return pl.ds(pl.multiple_of(start, 16), size)

    flights = []
    for offset, size, _ in parts:
        source = grads.at[rows(others + offset, size)]
        flights.append([send(source, from_core.at[pl.ds(offset, size)], partner)])
    yield
    for p, (offset, size, axes) in enumerate(parts):
        finish(flights[p])
        here = pl.ds(offset, size)
        kept = grads[rows(mine + offset, size)].astype(F32)
        half[here] = (kept + from_core[here].astype(F32)).astype(BF16)
        flights[p] = []
        for k in steps:
            at, device = peer(axes[0], k)
            piece = half.at[rows(offset + at * (size // 4), size // 4)]
            flights[p].append(send(piece, part_buffers[4 * p].at[k - 1], device))
    yield
    for p, (offset, size, axes) in enumerate(parts):
        finish(flights[p])
        got, kept, _, _ = part_buffers[4 * p : 4 * p + 4]
        total = half[rows(offset + spot[axes[0]] * (size // 4), size // 4)].astype(F32)
        for k in steps:
            total = total + got[k - 1].astype(F32)
        kept[...] = total
        flights[p] = []
        for k in steps:
            at, device = peer(axes[1], k)
            piece = kept.at[rows(at * (size // 16), size // 16)]
            flights[p].append(send(piece, part_buffers[4 * p + 2].at[k - 1], device))
    yield
    for p, (offset, size, axes) in enumerate(parts):
        finish(flights[p])
        _, kept, got, line = part_buffers[4 * p : 4 * p + 4]
        total = kept[rows(spot[axes[1]] * (size // 16), size // 16)]
        for k in steps:
            total = total + got[k - 1]
        piece = line.at[spot[axes[2]]]
        piece[...] = total
        flights[p] = [send(piece, piece, peer(axes[2], k)[1]) for k in steps]
    yield
    for p, (offset, size, axes) in enumerate(parts):
        finish(flights[p])
        line = part_buffers[4 * p + 3]
        start = mine + offset + spot[axes[0]] * (size // 4) + spot[axes[1]] * (size // 16)
        here = rows(start, size // 16)
        final[here] = (line[0] + line[1] + line[2] + line[3]).astype(BF16)
        piece = final.at[here]
        flights[p] = [send(piece, piece, peer(axes[1], k)[1]) for k in steps]
    yield
    for p, (offset, size, axes) in enumerate(parts):
        finish(flights[p])
        piece = final.at[rows(mine + offset + spot[axes[0]] * (size // 4), size // 4)]
        flights[p] = [send(piece, piece, peer(axes[0], k)[1]) for k in steps]
    yield
    for p, (offset, size, axes) in enumerate(parts):
        finish(flights[p])
        piece = final.at[rows(mine + offset, size)]
        flights[p] = [send(piece, piece, partner)]
    yield
    for flight in flights:
        finish(flight)
    yield


def total_buffers(parts):
    count = sum(size for _, size, _ in parts)
    buffers = [pltpu.VMEM((count, C), BF16)] * 2
    for _, size, _ in parts:
        buffers.append(pltpu.VMEM((3, size // 4, C), BF16))
        buffers.append(pltpu.VMEM((size // 4, C), F32))
        buffers.append(pltpu.VMEM((3, size // 16, C), F32))
        buffers.append(pltpu.VMEM((4, size // 16, C), F32))
    return buffers


PARTS_ONE = ((0, 512, "xzy"), (512, 512, "zyx"), (1024, 512, "yxz"))
PARTS_TWO = ((0, 768, "zxy"), (768, 512, "xyz"), (1280, 512, "yzx"))
ROWS_ONE = 2 * 1536
ROWS_TWO = 2 * 1792


def third_kernel(
    info, order,
    vol, faces, corners, slopes_two,
    own_mid, x_halo_mid, y_halo_mid, c_halo_mid, own_in, x_halo_in, y_halo_in, c_halo_in,
    gates, taps, results, c_in,
    final, arrived,
    grads, wide, wide_other, band, even, odd, sums, slopes, y_halo, c_halo,
    send_sem, recv_sem, sems, sems_other, *buffers,
):
    x, y = lax.axis_index("gx"), lax.axis_index("gy")
    core, chip = lax.rem(y, 2), y // 2
    inner = pl.ds(C, LINE)
    x_halo = [wide.at[17 * end, pl.ds(1, 2), :, inner] for end in range(2)]
    plan = halo_plan((vol.at[0], vol.at[15]), faces, corners, x_halo, y_halo, c_halo)
    devices = [device for _, _, device in plan] + [(x, y + 1 - 2 * core)]
    for k in range(1, 4):
        devices.append((4 * lax.rem(x // 4 + k, 4) + lax.rem(x, 4), y))
        devices.append((4 * (x // 4) + lax.rem(x + k, 4), y))
        devices.append((x, 2 * lax.rem(chip + k, 4) + core))
    workers = [lax.rem(x + k, 16) for k in range(1, 16)]
    devices += [(worker, y) for worker in workers]
    loads_mid = open_volume(own_mid, x_halo_mid, wide_other, sems_other)
    loads = open_volume(vol, None, wide, sems)
    moves = [pltpu.make_async_copy(results.at[x], arrived.at[x], sems.at[1])]
    moves[0].start()
    greet(devices)
    send = sender_of(send_sem, recv_sem)
    halo = [send(*item) for item in plan]
    for worker in workers:
        moves.append(send(results.at[worker], arrived.at[x], (worker, y)))
    buffers_one, buffers_two = buffers[: len(buffers) // 2], buffers[len(buffers) // 2 :]
    total_one = total_of(grads, final, 0, PARTS_ONE, send, buffers_one)
    total_two = total_of(grads, final, ROWS_ONE, PARTS_TWO, send, buffers_two)
    half = 16 // GROUP // 2

    def tap_sums(source):
        def act(number, members):
            for g, (_, place, _, _) in enumerate(members):
                cut_patch(wide_other, coords(place), even.at[g], odd.at[g])
            rows = source[pl.ds(number * GROUP, GROUP)].reshape(GROUP * 256, 2 * C)
            add_taps(sums, rows, even, odd)

        return act

    def back(number, members):
        for g, (_, place, _, _) in enumerate(members):
            cut_patch(wide, coords(place), even.at[g], odd.at[g])
        both = convolve(even, odd, band)
        for g, (position, _, _, live) in enumerate(members):
            rows = both[256 * g : 256 * g + 256] * gates[position].astype(F32)
            slopes[position] = jnp.where(live, rows, 0.0).astype(BF16)

    def clear(first, last):
        grads[first:last] = jnp.zeros((last - first, C), BF16)

    fill_band(band, taps, mirrored=True)
    sums[...] = jnp.zeros(sums.shape, F32)
    clear(27 * c_in, ROWS_ONE)
    clear(ROWS_ONE + 27 * C, ROWS_ONE + ROWS_TWO)
    close_volume(y_halo_mid, c_halo_mid, wide_other, loads_mid)
    groups(info, order, tap_sums(slopes_two), 0, 2 * half)
    gather_taps(sums, grads, C, ROWS_ONE)
    next(total_two)

    loads_in = open_volume(own_in, x_halo_in, wide_other, sems_other)
    sums[...] = jnp.zeros(sums.shape, F32)
    finish(halo)
    close_volume(y_halo, c_halo, wide, loads)
    groups(info, order, back, 0, half)
    next(total_two)
    groups(info, order, back, half, 2 * half)
    next(total_two)
    close_volume(y_halo_in, c_halo_in, wide_other, loads_in)
    groups(info, order, tap_sums(slopes), 0, half)
    next(total_two)
    groups(info, order, tap_sums(slopes), half, 2 * half)
    next(total_two)
    gather_taps(sums, grads, c_in, 0)
    next(total_one)
    for _ in range(3):
        next(total_two)
        next(total_one)
    for _ in range(4):
        next(total_one)
    finish(moves)


def finish_kernel(sender, grads, arrived, result, grad_one, grad_two):
    for number in range(result.shape[0]):
        result[number] = arrived[sender[number]]
    first = 0
    for out in (grad_one, grad_two):
        rows = grads[first : first + out.shape[0]].astype(F32)
        out[...] = rows * lax.rsqrt(jnp.mean(rows * rows) + 1e-05)
        first += ROWS_ONE


WIDE_SCRATCH = pltpu.VMEM((18, 4, 8, WIDE), BF16)
BAND_SCRATCH = pltpu.VMEM((9, 4 * C, 2 * C), BF16)
EVEN_SCRATCH = pltpu.VMEM((GROUP, 3, 80, PATCH), BF16)
ODD_SCRATCH = pltpu.VMEM((GROUP, 3, 64, PATCH), BF16)
SLOPES_SCRATCH = pltpu.VMEM((16, 256, 2 * C), BF16)
SUMS_SCRATCH = pltpu.VMEM((9, 2 * C, 4 * C), F32)
SEMS = pltpu.SemaphoreType.DMA((3,))
PARAMS = pltpu.CompilerParams(vmem_limit_bytes=LIMIT)


def body(
    features,
    voxel_mask,
    occupancy,
    send_counts,
    weight_one,
    bias_one,
    weight_two,
    bias_two,
    cotangent,
):
    c_in = weight_one.shape[1]
    mask = voxel_mask[0, 0].reshape(16, 64, 8).astype(F32)
    *vol_in, cots, info, order, sender = pl.pallas_call(
        volume_kernel,
        out_shape=(
            VOLUME,
            FACES,
            CORNERS,
            jax.ShapeDtypeStruct((16, 8, 8, BRICK), BF16),
            jax.ShapeDtypeStruct((49,), jnp.int32),
            jax.ShapeDtypeStruct((33,), jnp.int32),
            jax.ShapeDtypeStruct((9,), jnp.int32),
        ),
        in_specs=[SMEM, SMEM, VMEM, VMEM, VMEM],
        out_specs=(VMEM,) * 4 + (SMEM,) * 3,
        compiler_params=PARAMS,
        name="volume",
    )(occupancy, send_counts, features[0, 0], mask, cotangent[0, 0])
    halo_in = halo_exchange(*vol_in, 0)
    halo_in, cots = lax.optimization_barrier((halo_in, cots))
    cots = lax.all_to_all(cots, "gx", split_axis=0, concat_axis=0, tiled=True)

    *hidden, gates = pl.pallas_call(
        first_kernel,
        out_shape=(VOLUME, FACES, CORNERS, jax.ShapeDtypeStruct((16, 256, 2 * C), BF16)),
        in_specs=[SMEM, SMEM, ANY, ANY, VMEM, VMEM, VMEM, VMEM, VMEM],
        out_specs=(VMEM,) * 4,
        scratch_shapes=[WIDE_SCRATCH, BAND_SCRATCH, EVEN_SCRATCH, ODD_SCRATCH, SEMS],
        compiler_params=PARAMS,
        cost_estimate=pl.CostEstimate(flops=11 * 10**9, bytes_accessed=10**8, transcendentals=0),
        name="first",
    )(info, order, vol_in[0], *halo_in, mask, weight_one, jnp.tile(bias_one, 2)[None])
    halo_mid = halo_exchange(*hidden, 1)

    *edge, results, slopes = pl.pallas_call(
        second_kernel,
        out_shape=(
            VOLUME,
            FACES,
            CORNERS,
            jax.ShapeDtypeStruct((16, 8, 8, BRICK), BF16),
            jax.ShapeDtypeStruct((16, 256, 2 * C), BF16),
        ),
        in_specs=[SMEM, SMEM, ANY, ANY, VMEM, VMEM, VMEM, VMEM, VMEM, VMEM],
        out_specs=(VMEM,) * 5,
        scratch_shapes=[WIDE_SCRATCH, BAND_SCRATCH, EVEN_SCRATCH, ODD_SCRATCH, SEMS],
        compiler_params=PARAMS,
        name="second",
    )(info, order, hidden[0], *halo_mid, mask, weight_two, jnp.tile(bias_two, 2)[None], cots)
    grads, arrived = pl.pallas_call(
        lambda *refs: third_kernel(*refs[:17], c_in, *refs[17:]),
        out_shape=(
            jax.ShapeDtypeStruct((ROWS_ONE + ROWS_TWO, C), BF16),
            jax.ShapeDtypeStruct((16, 8, 8, BRICK), BF16),
        ),
        in_specs=[SMEM, SMEM, ANY, ANY, ANY, VMEM]
        + [ANY, ANY, VMEM, VMEM, ANY, ANY, VMEM, VMEM]
        + [VMEM, VMEM, ANY],
        out_specs=(VMEM, ANY),
        scratch_shapes=[
            pltpu.VMEM((ROWS_ONE + ROWS_TWO, C), BF16),
            WIDE_SCRATCH, WIDE_SCRATCH, BAND_SCRATCH, EVEN_SCRATCH, ODD_SCRATCH, SUMS_SCRATCH,
            SLOPES_SCRATCH, pltpu.VMEM(FACES.shape, BF16), pltpu.VMEM(CORNERS.shape, BF16),
            pltpu.SemaphoreType.DMA((128,)), pltpu.SemaphoreType.DMA((128,)), SEMS, SEMS,
            *total_buffers(PARTS_ONE), *total_buffers(PARTS_TWO),
        ],
        compiler_params=pltpu.CompilerParams(
            collective_id=3, has_side_effects=True, vmem_limit_bytes=LIMIT
        ),
        cost_estimate=pl.CostEstimate(flops=33 * 10**9, bytes_accessed=10**8, transcendentals=0),
        name="third",
    )(info, order, *edge, slopes, hidden[0], *halo_mid, vol_in[0], *halo_in, gates, weight_two, results)

    result, grad_one, grad_two = pl.pallas_call(
        finish_kernel,
        out_shape=(
            jax.ShapeDtypeStruct((8, 8, 8, BRICK), BF16),
            jax.ShapeDtypeStruct((27 * c_in, C), F32),
            jax.ShapeDtypeStruct((27 * C, C), F32),
        ),
        in_specs=[SMEM, VMEM, VMEM],
        out_specs=(VMEM,) * 3,
        compiler_params=PARAMS,
        name="finish",
    )(sender, grads, arrived)
    return (
        result[None, None],
        grad_one.reshape(weight_one.shape),
        grad_two.reshape(weight_two.shape),
    )


def solution(mesh):
    placed = (
        P("gx", "gy", None, None, None, None),
        P("gx", "gy", None, None),
        P("gx", "gy", None),
        P("gy", None, None),
        P(),
        P(),
        P(),
        P(),
        P("gx", "gy", None, None, None, None),
    )
    return jax.shard_map(
        body,
        mesh=mesh,
        in_specs=placed,
        out_specs=(P("gx", "gy", None, None, None, None), P(), P()),
        check_vma=False,
    )
```

```python
import functools

import jax
import jax.numpy as jnp
from jax import lax
from jax.experimental import pallas as pl
from jax.experimental.pallas import tpu as pltpu
from jax.sharding import PartitionSpec as P

MESH = pl.DeviceIdType.MESH
F32 = jnp.float32
BF16 = jnp.bfloat16
GROUP = 2
C = 128
BRICK = 8 * C
LINE = 8 * BRICK
WIDE = LINE + 2 * C
PATCH = BRICK + 2 * C
LIMIT = 60 * 1024 * 1024

VMEM = pl.BlockSpec(memory_space=pltpu.VMEM)
SMEM = pl.BlockSpec(memory_space=pltpu.SMEM)
ANY = pl.BlockSpec(memory_space=pl.ANY)

VOLUME = jax.ShapeDtypeStruct((16, 2, 8, LINE), BF16)
FACES = jax.ShapeDtypeStruct((2, 2, 8, LINE), BF16)
CORNERS = jax.ShapeDtypeStruct((4, 8, BRICK), BF16)


def coords(place):
    return lax.div(place, 16), lax.rem(lax.div(place, 8), 2), lax.rem(place, 8)


def put(vol, faces, spot, lane, value):
    xb, yb, zb = spot
    lanes = pl.ds(pl.multiple_of(zb * BRICK + lane, C), value.shape[2])
    vol[pl.ds(xb * 8, 8), yb, :, lanes] = value.astype(BF16)
    row = jnp.where(yb == 0, value[:, 0, :], value[:, 7, :])
    faces[yb, xb, :, lanes] = row.astype(BF16)


def put_corners(faces, corners):
    for side_y in range(2):
        for side_x in range(2):
            face = faces[side_y, side_x].astype(F32)
            row = face[7 * side_x : 7 * side_x + 1]
            rows = [row[:, z * BRICK : (z + 1) * BRICK] for z in range(8)]
            corners[2 * side_y + side_x] = jnp.concatenate(rows, axis=0).astype(BF16)


def volume_kernel(
    occupancy, counts, feat, mask, cotangent,
    vol, faces, corners, cots, info, order, sender,
):
    x = lax.axis_index("gx")

    def sort(place, numbers):
        active, empty = numbers
        xb, yb, zb = coords(place)
        slot = occupancy[xb, yb, zb]
        info[place] = slot
        live = slot >= 0
        order[jnp.where(live, active, 31 - empty)] = place
        one = live.astype(jnp.int32)
        return active + one, empty + 1 - one

    order[32] = lax.fori_loop(0, 32, sort, (0, 0))[0]

    def route(peer, numbers):
        slot, brick = numbers
        info[32 + slot] = peer
        sender[brick] = peer
        cots[peer] = cotangent[jnp.minimum(brick, 7)]
        return slot + counts[0, x, peer], brick + counts[0, peer, x]

    lax.fori_loop(0, 16, route, (0, 0))
    vol[...] = jnp.zeros(vol.shape, BF16)
    faces[...] = jnp.zeros(faces.shape, BF16)
    c_in = feat.shape[3] // 8

    def step(place, _):
        slot = info[place]

        @pl.when(slot >= 0)
        def _():
            rows = feat[slot].astype(F32)
            keep = mask[slot].reshape(8, 8, 8)
            pieces = []
            for w in range(8):
                pieces.append(rows[:, :, w * c_in : (w + 1) * c_in] * keep[:, :, w : w + 1])
                pieces.append(jnp.zeros((8, 8, C - c_in), F32))
            put(vol, faces, coords(place), 0, jnp.concatenate(pieces, axis=2))

        return 0

    lax.fori_loop(0, 32, step, 0)
    put_corners(faces, corners)


def halo_plan(x_faces, faces, corners, x_halo, y_halo, c_halo):
    nx, ny = lax.axis_size("gx"), lax.axis_size("gy")
    x, y = lax.axis_index("gx"), lax.axis_index("gy")
    left, right = lax.rem(x + nx - 1, nx), lax.rem(x + 1, nx)
    down, up = lax.rem(y + ny - 1, ny), lax.rem(y + 1, ny)
    return [
        (x_faces[0], x_halo[1], (left, y)),
        (x_faces[1], x_halo[0], (right, y)),
        (faces.at[0], y_halo.at[1], (x, down)),
        (faces.at[1], y_halo.at[0], (x, up)),
        (corners.at[0], c_halo.at[3], (left, down)),
        (corners.at[1], c_halo.at[2], (right, down)),
        (corners.at[2], c_halo.at[1], (left, up)),
        (corners.at[3], c_halo.at[0], (right, up)),
    ]


def greet(devices):
    barrier = pltpu.get_barrier_semaphore()
    for device in devices:
        pl.semaphore_signal(barrier, inc=1, device_id=device, device_id_type=MESH)
    pl.semaphore_wait(barrier, len(devices))


def sender_of(send_sem, recv_sem):
    used = iter(range(send_sem.shape[0]))

    def send(source, target, device):
        number = next(used)
        copy = pltpu.make_async_remote_copy(
            src_ref=source,
            dst_ref=target,
            send_sem=send_sem.at[number],
            recv_sem=recv_sem.at[number],
            device_id=device,
            device_id_type=MESH,
        )
        copy.start()
        return copy

    return send


def finish(copies):
    for copy in copies:
        copy.wait()


def halo_kernel(vol, faces, corners, x_halo, y_halo, c_halo, send_sem, recv_sem):
    x_faces = (vol.at[0], vol.at[15])
    plan = halo_plan(x_faces, faces, corners, (x_halo.at[0], x_halo.at[1]), y_halo, c_halo)
    greet([device for _, _, device in plan])
    send = sender_of(send_sem, recv_sem)
    finish([send(*item) for item in plan])


def halo_exchange(vol, faces, corners, number):
    return pl.pallas_call(
        halo_kernel,
        out_shape=(jax.ShapeDtypeStruct((2, 2, 8, LINE), BF16), FACES, CORNERS),
        in_specs=[ANY] * 3,
        out_specs=(ANY,) * 3,
        scratch_shapes=[pltpu.SemaphoreType.DMA((8,)), pltpu.SemaphoreType.DMA((8,))],
        compiler_params=pltpu.CompilerParams(collective_id=number, has_side_effects=True),
        name="halo",
    )(vol, faces, corners)


def inside_slab():
    x, y = lax.axis_index("gx"), lax.axis_index("gy")
    nx, ny = lax.axis_size("gx"), lax.axis_size("gy")
    return (x > 0, x < nx - 1), (y > 0, y < ny - 1)


def open_volume(own, x_halo, wide, sems):
    inner = pl.ds(C, LINE)
    copies = [pltpu.make_async_copy(own, wide.at[pl.ds(1, 16), pl.ds(1, 2), :, inner], sems.at[0])]
    if x_halo is not None:
        for end in range(2):
            target = wide.at[17 * end, pl.ds(1, 2), :, inner]
            copies.append(pltpu.make_async_copy(x_halo.at[end], target, sems.at[1 + end]))
    for copy in copies:
        copy.start()
    return copies


def close_volume(y_halo, c_halo, wide, copies):
    inside_x, inside_y = inside_slab()
    inner = pl.ds(C, LINE)
    margin = jnp.zeros((18, 4, 8, C), BF16)
    wide[:, :, :, 0:C] = margin
    wide[:, :, :, C + LINE : WIDE] = margin
    for side in range(2):
        block = 3 * side
        for half in range(2):
            face = jnp.where(inside_y[side], y_halo[side, half].astype(F32), 0.0)
            for row in range(8):
                wide[1 + 8 * half + row, block, :, inner] = jnp.broadcast_to(
                    face[row : row + 1], (8, LINE)
                ).astype(BF16)
        for end in range(2):
            inside = inside_y[side] & inside_x[end]
            corner = jnp.where(inside, c_halo[2 * side + end].astype(F32), 0.0)
            for z in range(8):
                wide[17 * end, block, :, pl.ds(C + z * BRICK, BRICK)] = jnp.broadcast_to(
                    corner[z : z + 1], (8, BRICK)
                ).astype(BF16)
    finish(copies)
    for end in range(2):

        @pl.when(jnp.logical_not(inside_x[end]))
        def _():
            wide[17 * end, 1:3, :, inner] = jnp.zeros((2, 8, LINE), BF16)


def cut_patch(wide, spot, even, odd):
    xb, yb, zb = spot
    lanes = pl.ds(zb * BRICK, PATCH)
    rows = pl.ds(xb * 8, 10)
    before = wide[rows, yb, :, lanes].astype(F32)
    here = wide[rows, yb + 1, :, lanes].astype(F32)
    after = wide[rows, yb + 2, :, lanes].astype(F32)
    line = lax.broadcasted_iota(jnp.int32, here.shape, 1)
    shifts = [
        pltpu.roll(jnp.where(line == 7, before, here), 1, 1),
        here,
        pltpu.roll(jnp.where(line == 0, after, here), 7, 1),
    ]
    for b in range(3):
        even[b] = shifts[b].reshape(80, PATCH).astype(BF16)
        odd[b] = shifts[b][1:9].reshape(64, PATCH).astype(BF16)


def window(even, odd, a, b):
    parts = []
    for g in range(GROUP):
        for j in range(4):
            lanes = pl.ds(2 * C * j, 4 * C)
            parts.append(odd[g, b, :, lanes] if a == 1 else even[g, b, pl.ds(8 * a, 64), lanes])
    return jnp.concatenate(parts, axis=0)


def fill_band(band, taps, mirrored=False):
    depth = taps.shape[1]
    band[...] = jnp.zeros(band.shape, BF16)
    for tap in range(9):
        for c in range(3):
            block = taps[26 - 3 * tap - c].T if mirrored else taps[3 * tap + c]
            for o in range(2):
                band[tap, pl.ds((c + o) * C, depth), pl.ds(o * C, C)] = block


def convolve(even, odd, band):
    total = jnp.zeros((GROUP * 256, 2 * C), F32)
    for a in range(3):
        for b in range(3):
            total = total + jnp.dot(
                window(even, odd, a, b), band[3 * a + b], preferred_element_type=F32
            )
    return total


def add_taps(sums, slopes, even, odd):
    turned = slopes.astype(F32).T.astype(BF16)
    for a in range(3):
        for b in range(3):
            sums[3 * a + b] += jnp.dot(
                turned, window(even, odd, a, b), preferred_element_type=F32
            )


def gather_taps(sums, grad, depth, first):
    for tap in range(9):
        for c in range(3):
            part = (
                sums[tap, 0:C, c * C : (c + 1) * C]
                + sums[tap, C : 2 * C, (c + 1) * C : (c + 2) * C]
            )
            grad[pl.ds(first + (3 * tap + c) * depth, depth)] = part.T[0:depth].astype(BF16)


def groups(info, order, act, start, stop):
    def step(number, _):
        members = []
        for g in range(GROUP):
            position = number * GROUP + g
            place = order[position]
            slot = info[place]
            members.append((position, place, jnp.maximum(slot, 0), slot >= 0))
        act(number, members)
        return 0

    lax.fori_loop(start, stop, step, 0)


def all_groups(info, order, act):
    groups(info, order, act, 0, (order[32] + GROUP - 1) // GROUP)


def spread_mask(keep):
    blocks = []
    for j in range(4):
        pair = [jnp.broadcast_to(keep[:, 2 * j + o : 2 * j + o + 1], (64, C)) for o in range(2)]
        blocks.append(jnp.concatenate(pair, axis=1))
    return jnp.concatenate(blocks, axis=0)


def sigmoid(value):
    return 1.0 / (1.0 + jnp.exp(-value))


def first_kernel(
    info, order, own, x_halo, y_halo, c_halo, mask, taps, bias,
    vol, faces, corners, gates,
    wide, band, even, odd, sems,
):
    copies = open_volume(own, x_halo, wide, sems)
    fill_band(band, taps)
    vol[...] = jnp.zeros(vol.shape, BF16)
    faces[...] = jnp.zeros(faces.shape, BF16)

    def forward(number, members):
        for g, (_, place, _, _) in enumerate(members):
            cut_patch(wide, coords(place), even.at[g], odd.at[g])
        both = convolve(even, odd, band) + bias[...]
        for g, (position, place, slot, live) in enumerate(members):
            linear = both[256 * g : 256 * g + 256]
            keep = jnp.where(live, spread_mask(mask[slot]), 0.0)
            sig = sigmoid(linear)
            hidden = keep * (linear * sig)
            gates[position] = (keep * (sig * (1.0 + linear * (1.0 - sig)))).astype(BF16)
            for j in range(4):
                piece = hidden[64 * j : 64 * j + 64].reshape(8, 8, 2 * C)
                put(vol, faces, coords(place), 2 * C * j, piece)

    close_volume(y_halo, c_halo, wide, copies)
    all_groups(info, order, forward)
    put_corners(faces, corners)


def second_kernel(
    info, order, own, x_halo, y_halo, c_halo, mask, taps, bias, cots,
    vol, faces, corners, results, slopes,
    wide, band, even, odd, sems,
):
    copies = open_volume(own, x_halo, wide, sems)
    fill_band(band, taps)
    vol[...] = jnp.zeros(vol.shape, BF16)
    faces[...] = jnp.zeros(faces.shape, BF16)
    slopes[...] = jnp.zeros(slopes.shape, BF16)

    def forward(number, members):
        for g, (_, place, _, _) in enumerate(members):
            cut_patch(wide, coords(place), even.at[g], odd.at[g])
        both = convolve(even, odd, band) + bias[...]
        for g, (position, place, slot, live) in enumerate(members):
            worker = info[32 + slot]
            linear = both[256 * g : 256 * g + 256]
            keep = jnp.where(live, spread_mask(mask[slot]), 0.0)
            sig = sigmoid(linear)
            output = keep * (linear * sig)
            slope = keep * (sig * (1.0 + linear * (1.0 - sig)))
            for j in range(4):
                rows = slice(64 * j, 64 * j + 64)
                lanes = pl.ds(2 * C * j, 2 * C)
                piece = cots[worker, :, :, lanes].astype(F32).reshape(64, 2 * C) * slope[rows]
                slopes[position, pl.ds(64 * j, 64)] = piece.astype(BF16)
                put(vol, faces, coords(place), 2 * C * j, piece.reshape(8, 8, 2 * C))

            @pl.when(live)
            def _():
                for j in range(4):
                    rows = output[64 * j : 64 * j + 64].reshape(8, 8, 2 * C)
                    results[worker, :, :, pl.ds(2 * C * j, 2 * C)] = rows.astype(BF16)

    close_volume(y_halo, c_halo, wide, copies)
    all_groups(info, order, forward)
    put_corners(faces, corners)


def total_of(grads, final, base, parts, send, buffers):
    x, y = lax.axis_index("gx"), lax.axis_index("gy")
    core = lax.rem(y, 2)
    spot = {"x": x // 4, "z": lax.rem(x, 4), "y": y // 2}
    partner = (x, y + 1 - 2 * core)
    steps = range(1, 4)
    from_core, half, *part_buffers = buffers
    count = half.shape[0]
    mine, others = base + core * count, base + (1 - core) * count

    def peer(axis, k):
        at = lax.rem(spot[axis] + k, 4)
        if axis == "x":
            return at, (4 * at + spot["z"], y)
        if axis == "z":
            return at, (4 * spot["x"] + at, y)
        return at, (x, 2 * at + core)

    def rows(start, size):
        return pl.ds(pl.multiple_of(start, 16), size)

    flights = []
    for offset, size, _ in parts:
        source = grads.at[rows(others + offset, size)]
        flights.append([send(source, from_core.at[pl.ds(offset, size)], partner)])
    yield
    for p, (offset, size, axes) in enumerate(parts):
        finish(flights[p])
        here = pl.ds(offset, size)
        kept = grads[rows(mine + offset, size)].astype(F32)
        half[here] = (kept + from_core[here].astype(F32)).astype(BF16)
        flights[p] = []
        for k in steps:
            at, device = peer(axes[0], k)
            piece = half.at[rows(offset + at * (size // 4), size // 4)]
            flights[p].append(send(piece, part_buffers[4 * p].at[k - 1], device))
    yield
    for p, (offset, size, axes) in enumerate(parts):
        finish(flights[p])
        got, kept, _, _ = part_buffers[4 * p : 4 * p + 4]
        total = half[rows(offset + spot[axes[0]] * (size // 4), size // 4)].astype(F32)
        for k in steps:
            total = total + got[k - 1].astype(F32)
        kept[...] = total
        flights[p] = []
        for k in steps:
            at, device = peer(axes[1], k)
            piece = kept.at[rows(at * (size // 16), size // 16)]
            flights[p].append(send(piece, part_buffers[4 * p + 2].at[k - 1], device))
    yield
    for p, (offset, size, axes) in enumerate(parts):
        finish(flights[p])
        _, kept, got, line = part_buffers[4 * p : 4 * p + 4]
        total = kept[rows(spot[axes[1]] * (size // 16), size // 16)]
        for k in steps:
            total = total + got[k - 1]
        piece = line.at[spot[axes[2]]]
        piece[...] = total
        flights[p] = [send(piece, piece, peer(axes[2], k)[1]) for k in steps]
    yield
    for p, (offset, size, axes) in enumerate(parts):
        finish(flights[p])
        line = part_buffers[4 * p + 3]
        start = mine + offset + spot[axes[0]] * (size // 4) + spot[axes[1]] * (size // 16)
        here = rows(start, size // 16)
        final[here] = (line[0] + line[1] + line[2] + line[3]).astype(BF16)
        piece = final.at[here]
        flights[p] = [send(piece, piece, peer(axes[1], k)[1]) for k in steps]
    yield
    for p, (offset, size, axes) in enumerate(parts):
        finish(flights[p])
        piece = final.at[rows(mine + offset + spot[axes[0]] * (size // 4), size // 4)]
        flights[p] = [send(piece, piece, peer(axes[0], k)[1]) for k in steps]
    yield
    for p, (offset, size, axes) in enumerate(parts):
        finish(flights[p])
        piece = final.at[rows(mine + offset, size)]
        flights[p] = [send(piece, piece, partner)]
    yield
    for flight in flights:
        finish(flight)
    yield


def total_buffers(parts):
    count = sum(size for _, size, _ in parts)
    buffers = [pltpu.VMEM((count, C), BF16)] * 2
    for _, size, _ in parts:
        buffers.append(pltpu.VMEM((3, size // 4, C), BF16))
        buffers.append(pltpu.VMEM((size // 4, C), F32))
        buffers.append(pltpu.VMEM((3, size // 16, C), F32))
        buffers.append(pltpu.VMEM((4, size // 16, C), F32))
    return buffers


PARTS_ONE = ((0, 512, "xzy"), (512, 512, "zyx"), (1024, 512, "yxz"))
PARTS_TWO = ((0, 768, "zxy"), (768, 512, "xyz"), (1280, 512, "yzx"))
ROWS_ONE = 2 * 1536
ROWS_TWO = 2 * 1792


def third_kernel(
    info, order,
    vol, faces, corners, slopes_two,
    own_mid, x_halo_mid, y_halo_mid, c_halo_mid, own_in, x_halo_in, y_halo_in, c_halo_in,
    gates, taps, results, c_in,
    final, arrived,
    grads, wide, wide_other, band, even, odd, sums, slopes, y_halo, c_halo,
    send_sem, recv_sem, sems, sems_other, *buffers,
):
    x, y = lax.axis_index("gx"), lax.axis_index("gy")
    core, chip = lax.rem(y, 2), y // 2
    inner = pl.ds(C, LINE)
    x_halo = [wide.at[17 * end, pl.ds(1, 2), :, inner] for end in range(2)]
    plan = halo_plan((vol.at[0], vol.at[15]), faces, corners, x_halo, y_halo, c_halo)
    devices = [device for _, _, device in plan] + [(x, y + 1 - 2 * core)]
    for k in range(1, 4):
        devices.append((4 * lax.rem(x // 4 + k, 4) + lax.rem(x, 4), y))
        devices.append((4 * (x // 4) + lax.rem(x + k, 4), y))
        devices.append((x, 2 * lax.rem(chip + k, 4) + core))
    workers = [lax.rem(x + k, 16) for k in range(1, 16)]
    devices += [(worker, y) for worker in workers]
    loads_mid = open_volume(own_mid, x_halo_mid, wide_other, sems_other)
    loads = open_volume(vol, None, wide, sems)
    moves = [pltpu.make_async_copy(results.at[x], arrived.at[x], sems.at[1])]
    moves[0].start()
    greet(devices)
    send = sender_of(send_sem, recv_sem)
    halo = [send(*item) for item in plan]
    for worker in workers:
        moves.append(send(results.at[worker], arrived.at[x], (worker, y)))
    buffers_one, buffers_two = buffers[: len(buffers) // 2], buffers[len(buffers) // 2 :]
    total_one = total_of(grads, final, 0, PARTS_ONE, send, buffers_one)
    total_two = total_of(grads, final, ROWS_ONE, PARTS_TWO, send, buffers_two)
    count = 16 // GROUP

    def tap_sums(source):
        def act(number, members):
            for g, (_, place, _, _) in enumerate(members):
                cut_patch(wide_other, coords(place), even.at[g], odd.at[g])
            rows = source[pl.ds(number * GROUP, GROUP)].reshape(GROUP * 256, 2 * C)
            add_taps(sums, rows, even, odd)

        return act

    def back(number, members):
        for g, (_, place, _, _) in enumerate(members):
            cut_patch(wide, coords(place), even.at[g], odd.at[g])
        both = convolve(even, odd, band)
        for g, (position, _, _, live) in enumerate(members):
            rows = both[256 * g : 256 * g + 256] * gates[position].astype(F32)
            slopes[position] = jnp.where(live, rows, 0.0).astype(BF16)

    def clear(first, last):
        grads[first:last] = jnp.zeros((last - first, C), BF16)

    fill_band(band, taps, mirrored=True)
    sums[...] = jnp.zeros(sums.shape, F32)
    clear(27 * c_in, ROWS_ONE)
    clear(ROWS_ONE + 27 * C, ROWS_ONE + ROWS_TWO)
    close_volume(y_halo_mid, c_halo_mid, wide_other, loads_mid)
    groups(info, order, tap_sums(slopes_two), 0, count)
    gather_taps(sums, grads, C, ROWS_ONE)
    next(total_two)

    loads_in = open_volume(own_in, x_halo_in, wide_other, sems_other)
    sums[...] = jnp.zeros(sums.shape, F32)
    finish(halo)
    close_volume(y_halo, c_halo, wide, loads)
    groups(info, order, back, 0, count)
    next(total_two)
    close_volume(y_halo_in, c_halo_in, wide_other, loads_in)
    groups(info, order, tap_sums(slopes), 0, count)
    gather_taps(sums, grads, c_in, 0)
    for _ in range(6):
        next(total_one)
        next(total_two)
    next(total_one)
    next(total_one)
    finish(moves)


def finish_kernel(sender, grads, arrived, result, grad_one, grad_two):
    for number in range(result.shape[0]):
        result[number] = arrived[sender[number]]
    first = 0
    for out in (grad_one, grad_two):
        rows = grads[first : first + out.shape[0]].astype(F32)
        out[...] = rows * lax.rsqrt(jnp.mean(rows * rows) + 1e-05)
        first += ROWS_ONE


WIDE_SCRATCH = pltpu.VMEM((18, 4, 8, WIDE), BF16)
BAND_SCRATCH = pltpu.VMEM((9, 4 * C, 2 * C), BF16)
EVEN_SCRATCH = pltpu.VMEM((GROUP, 3, 80, PATCH), BF16)
ODD_SCRATCH = pltpu.VMEM((GROUP, 3, 64, PATCH), BF16)
SLOPES_SCRATCH = pltpu.VMEM((16, 256, 2 * C), BF16)
SUMS_SCRATCH = pltpu.VMEM((9, 2 * C, 4 * C), F32)
SEMS = pltpu.SemaphoreType.DMA((3,))
PARAMS = pltpu.CompilerParams(vmem_limit_bytes=LIMIT)


def body(
    features,
    voxel_mask,
    occupancy,
    send_counts,
    weight_one,
    bias_one,
    weight_two,
    bias_two,
    cotangent,
):
    c_in = weight_one.shape[1]
    mask = voxel_mask[0, 0].reshape(16, 64, 8).astype(F32)
    *vol_in, cots, info, order, sender = pl.pallas_call(
        volume_kernel,
        out_shape=(
            VOLUME,
            FACES,
            CORNERS,
            jax.ShapeDtypeStruct((16, 8, 8, BRICK), BF16),
            jax.ShapeDtypeStruct((49,), jnp.int32),
            jax.ShapeDtypeStruct((33,), jnp.int32),
            jax.ShapeDtypeStruct((9,), jnp.int32),
        ),
        in_specs=[SMEM, SMEM, VMEM, VMEM, VMEM],
        out_specs=(VMEM,) * 4 + (SMEM,) * 3,
        compiler_params=PARAMS,
        name="volume",
    )(occupancy, send_counts, features[0, 0], mask, cotangent[0, 0])
    halo_in = halo_exchange(*vol_in, 0)
    halo_in, cots = lax.optimization_barrier((halo_in, cots))
    cots = lax.all_to_all(cots, "gx", split_axis=0, concat_axis=0, tiled=True)

    *hidden, gates = pl.pallas_call(
        first_kernel,
        out_shape=(VOLUME, FACES, CORNERS, jax.ShapeDtypeStruct((16, 256, 2 * C), BF16)),
        in_specs=[SMEM, SMEM, ANY, ANY, VMEM, VMEM, VMEM, VMEM, VMEM],
        out_specs=(VMEM,) * 4,
        scratch_shapes=[WIDE_SCRATCH, BAND_SCRATCH, EVEN_SCRATCH, ODD_SCRATCH, SEMS],
        compiler_params=PARAMS,
        cost_estimate=pl.CostEstimate(flops=11 * 10**9, bytes_accessed=10**8, transcendentals=0),
        name="first",
    )(info, order, vol_in[0], *halo_in, mask, weight_one, jnp.tile(bias_one, 2)[None])
    halo_mid = halo_exchange(*hidden, 1)

    *edge, results, slopes = pl.pallas_call(
        second_kernel,
        out_shape=(
            VOLUME,
            FACES,
            CORNERS,
            jax.ShapeDtypeStruct((16, 8, 8, BRICK), BF16),
            jax.ShapeDtypeStruct((16, 256, 2 * C), BF16),
        ),
        in_specs=[SMEM, SMEM, ANY, ANY, VMEM, VMEM, VMEM, VMEM, VMEM, VMEM],
        out_specs=(VMEM,) * 5,
        scratch_shapes=[WIDE_SCRATCH, BAND_SCRATCH, EVEN_SCRATCH, ODD_SCRATCH, SEMS],
        compiler_params=PARAMS,
        name="second",
    )(info, order, hidden[0], *halo_mid, mask, weight_two, jnp.tile(bias_two, 2)[None], cots)
    grads, arrived = pl.pallas_call(
        lambda *refs: third_kernel(*refs[:17], c_in, *refs[17:]),
        out_shape=(
            jax.ShapeDtypeStruct((ROWS_ONE + ROWS_TWO, C), BF16),
            jax.ShapeDtypeStruct((16, 8, 8, BRICK), BF16),
        ),
        in_specs=[SMEM, SMEM, ANY, ANY, ANY, VMEM]
        + [ANY, ANY, VMEM, VMEM, ANY, ANY, VMEM, VMEM]
        + [VMEM, VMEM, ANY],
        out_specs=(VMEM, ANY),
        scratch_shapes=[
            pltpu.VMEM((ROWS_ONE + ROWS_TWO, C), BF16),
            WIDE_SCRATCH, WIDE_SCRATCH, BAND_SCRATCH, EVEN_SCRATCH, ODD_SCRATCH, SUMS_SCRATCH,
            SLOPES_SCRATCH, pltpu.VMEM(FACES.shape, BF16), pltpu.VMEM(CORNERS.shape, BF16),
            pltpu.SemaphoreType.DMA((128,)), pltpu.SemaphoreType.DMA((128,)), SEMS, SEMS,
            *total_buffers(PARTS_ONE), *total_buffers(PARTS_TWO),
        ],
        compiler_params=pltpu.CompilerParams(
            collective_id=3, has_side_effects=True, vmem_limit_bytes=LIMIT
        ),
        cost_estimate=pl.CostEstimate(flops=33 * 10**9, bytes_accessed=10**8, transcendentals=0),
        name="third",
    )(info, order, *edge, slopes, hidden[0], *halo_mid, vol_in[0], *halo_in, gates, weight_two, results)

    result, grad_one, grad_two = pl.pallas_call(
        finish_kernel,
        out_shape=(
            jax.ShapeDtypeStruct((8, 8, 8, BRICK), BF16),
            jax.ShapeDtypeStruct((27 * c_in, C), F32),
            jax.ShapeDtypeStruct((27 * C, C), F32),
        ),
        in_specs=[SMEM, VMEM, VMEM],
        out_specs=(VMEM,) * 3,
        compiler_params=PARAMS,
        name="finish",
    )(sender, grads, arrived)
    return (
        result[None, None],
        grad_one.reshape(weight_one.shape),
        grad_two.reshape(weight_two.shape),
    )


def solution(mesh):
    placed = (
        P("gx", "gy", None, None, None, None),
        P("gx", "gy", None, None),
        P("gx", "gy", None),
        P("gy", None, None),
        P(),
        P(),
        P(),
        P(),
        P("gx", "gy", None, None, None, None),
    )
    return jax.shard_map(
        body,
        mesh=mesh,
        in_specs=placed,
        out_specs=(P("gx", "gy", None, None, None, None), P(), P()),
        check_vma=False,
    )
```

```python
import functools

import jax
import jax.numpy as jnp
from jax import lax
from jax.experimental import pallas as pl
from jax.experimental.pallas import tpu as pltpu
from jax.sharding import PartitionSpec as P

MESH = pl.DeviceIdType.MESH
F32 = jnp.float32
BF16 = jnp.bfloat16
GROUP = 4
C = 128
BRICK = 8 * C
LINE = 8 * BRICK
WIDE = LINE + 2 * C
PATCH = BRICK + 2 * C
LIMIT = 60 * 1024 * 1024

VMEM = pl.BlockSpec(memory_space=pltpu.VMEM)
SMEM = pl.BlockSpec(memory_space=pltpu.SMEM)
ANY = pl.BlockSpec(memory_space=pl.ANY)

VOLUME = jax.ShapeDtypeStruct((16, 2, 8, LINE), BF16)
FACES = jax.ShapeDtypeStruct((2, 2, 8, LINE), BF16)
CORNERS = jax.ShapeDtypeStruct((4, 8, BRICK), BF16)


def coords(place):
    return lax.div(place, 16), lax.rem(lax.div(place, 8), 2), lax.rem(place, 8)


def put(vol, faces, spot, lane, value):
    xb, yb, zb = spot
    lanes = pl.ds(pl.multiple_of(zb * BRICK + lane, C), value.shape[2])
    vol[pl.ds(xb * 8, 8), yb, :, lanes] = value.astype(BF16)
    row = jnp.where(yb == 0, value[:, 0, :], value[:, 7, :])
    faces[yb, xb, :, lanes] = row.astype(BF16)


def put_corners(faces, corners):
    for side_y in range(2):
        for side_x in range(2):
            face = faces[side_y, side_x].astype(F32)
            row = face[7 * side_x : 7 * side_x + 1]
            rows = [row[:, z * BRICK : (z + 1) * BRICK] for z in range(8)]
            corners[2 * side_y + side_x] = jnp.concatenate(rows, axis=0).astype(BF16)


def volume_kernel(
    occupancy, counts, feat, mask, cotangent,
    vol, faces, corners, cots, info, order, sender,
):
    x = lax.axis_index("gx")

    def sort(place, numbers):
        active, empty = numbers
        xb, yb, zb = coords(place)
        slot = occupancy[xb, yb, zb]
        info[place] = slot
        live = slot >= 0
        order[jnp.where(live, active, 31 - empty)] = place
        one = live.astype(jnp.int32)
        return active + one, empty + 1 - one

    order[32] = lax.fori_loop(0, 32, sort, (0, 0))[0]

    def route(peer, numbers):
        slot, brick = numbers
        info[32 + slot] = peer
        sender[brick] = peer
        cots[peer] = cotangent[jnp.minimum(brick, 7)]
        return slot + counts[0, x, peer], brick + counts[0, peer, x]

    lax.fori_loop(0, 16, route, (0, 0))
    vol[...] = jnp.zeros(vol.shape, BF16)
    faces[...] = jnp.zeros(faces.shape, BF16)
    c_in = feat.shape[3] // 8

    def step(place, _):
        slot = info[place]

        @pl.when(slot >= 0)
        def _():
            rows = feat[slot].astype(F32)
            keep = mask[slot].reshape(8, 8, 8)
            pieces = []
            for w in range(8):
                pieces.append(rows[:, :, w * c_in : (w + 1) * c_in] * keep[:, :, w : w + 1])
                pieces.append(jnp.zeros((8, 8, C - c_in), F32))
            put(vol, faces, coords(place), 0, jnp.concatenate(pieces, axis=2))

        return 0

    lax.fori_loop(0, 32, step, 0)
    put_corners(faces, corners)


def halo_plan(x_faces, faces, corners, x_halo, y_halo, c_halo):
    nx, ny = lax.axis_size("gx"), lax.axis_size("gy")
    x, y = lax.axis_index("gx"), lax.axis_index("gy")
    left, right = lax.rem(x + nx - 1, nx), lax.rem(x + 1, nx)
    down, up = lax.rem(y + ny - 1, ny), lax.rem(y + 1, ny)
    return [
        (x_faces[0], x_halo[1], (left, y)),
        (x_faces[1], x_halo[0], (right, y)),
        (faces.at[0], y_halo.at[1], (x, down)),
        (faces.at[1], y_halo.at[0], (x, up)),
        (corners.at[0], c_halo.at[3], (left, down)),
        (corners.at[1], c_halo.at[2], (right, down)),
        (corners.at[2], c_halo.at[1], (left, up)),
        (corners.at[3], c_halo.at[0], (right, up)),
    ]


def greet(devices):
    barrier = pltpu.get_barrier_semaphore()
    for device in devices:
        pl.semaphore_signal(barrier, inc=1, device_id=device, device_id_type=MESH)
    pl.semaphore_wait(barrier, len(devices))


def sender_of(send_sem, recv_sem):
    used = iter(range(send_sem.shape[0]))

    def send(source, target, device):
        number = next(used)
        copy = pltpu.make_async_remote_copy(
            src_ref=source,
            dst_ref=target,
            send_sem=send_sem.at[number],
            recv_sem=recv_sem.at[number],
            device_id=device,
            device_id_type=MESH,
        )
        copy.start()
        return copy

    return send


def finish(copies):
    for copy in copies:
        copy.wait()


def halo_kernel(vol, faces, corners, x_halo, y_halo, c_halo, send_sem, recv_sem):
    x_faces = (vol.at[0], vol.at[15])
    plan = halo_plan(x_faces, faces, corners, (x_halo.at[0], x_halo.at[1]), y_halo, c_halo)
    greet([device for _, _, device in plan])
    send = sender_of(send_sem, recv_sem)
    finish([send(*item) for item in plan])


def halo_exchange(vol, faces, corners, number):
    return pl.pallas_call(
        halo_kernel,
        out_shape=(jax.ShapeDtypeStruct((2, 2, 8, LINE), BF16), FACES, CORNERS),
        in_specs=[ANY] * 3,
        out_specs=(ANY,) * 3,
        scratch_shapes=[pltpu.SemaphoreType.DMA((8,)), pltpu.SemaphoreType.DMA((8,))],
        compiler_params=pltpu.CompilerParams(collective_id=number, has_side_effects=True),
        name="halo",
    )(vol, faces, corners)


def inside_slab():
    x, y = lax.axis_index("gx"), lax.axis_index("gy")
    nx, ny = lax.axis_size("gx"), lax.axis_size("gy")
    return (x > 0, x < nx - 1), (y > 0, y < ny - 1)


def open_volume(own, x_halo, wide, sems):
    inner = pl.ds(C, LINE)
    copies = [pltpu.make_async_copy(own, wide.at[pl.ds(1, 16), pl.ds(1, 2), :, inner], sems.at[0])]
    if x_halo is not None:
        for end in range(2):
            target = wide.at[17 * end, pl.ds(1, 2), :, inner]
            copies.append(pltpu.make_async_copy(x_halo.at[end], target, sems.at[1 + end]))
    for copy in copies:
        copy.start()
    return copies


def close_volume(y_halo, c_halo, wide, copies):
    inside_x, inside_y = inside_slab()
    inner = pl.ds(C, LINE)
    margin = jnp.zeros((18, 4, 8, C), BF16)
    wide[:, :, :, 0:C] = margin
    wide[:, :, :, C + LINE : WIDE] = margin
    for side in range(2):
        block = 3 * side
        for half in range(2):
            face = jnp.where(inside_y[side], y_halo[side, half].astype(F32), 0.0)
            for row in range(8):
                wide[1 + 8 * half + row, block, :, inner] = jnp.broadcast_to(
                    face[row : row + 1], (8, LINE)
                ).astype(BF16)
        for end in range(2):
            inside = inside_y[side] & inside_x[end]
            corner = jnp.where(inside, c_halo[2 * side + end].astype(F32), 0.0)
            for z in range(8):
                wide[17 * end, block, :, pl.ds(C + z * BRICK, BRICK)] = jnp.broadcast_to(
                    corner[z : z + 1], (8, BRICK)
                ).astype(BF16)
    finish(copies)
    for end in range(2):

        @pl.when(jnp.logical_not(inside_x[end]))
        def _():
            wide[17 * end, 1:3, :, inner] = jnp.zeros((2, 8, LINE), BF16)


def cut_patch(wide, spot, even, odd):
    xb, yb, zb = spot
    lanes = pl.ds(zb * BRICK, PATCH)
    rows = pl.ds(xb * 8, 10)
    before = wide[rows, yb, :, lanes].astype(F32)
    here = wide[rows, yb + 1, :, lanes].astype(F32)
    after = wide[rows, yb + 2, :, lanes].astype(F32)
    line = lax.broadcasted_iota(jnp.int32, here.shape, 1)
    shifts = [
        pltpu.roll(jnp.where(line == 7, before, here), 1, 1),
        here,
        pltpu.roll(jnp.where(line == 0, after, here), 7, 1),
    ]
    for b in range(3):
        even[b] = shifts[b].reshape(80, PATCH).astype(BF16)
        odd[b] = shifts[b][1:9].reshape(64, PATCH).astype(BF16)


def window(even, odd, a, b):
    parts = []
    for g in range(GROUP):
        for j in range(4):
            lanes = pl.ds(2 * C * j, 4 * C)
            parts.append(odd[g, b, :, lanes] if a == 1 else even[g, b, pl.ds(8 * a, 64), lanes])
    return jnp.concatenate(parts, axis=0)


def fill_band(band, taps, mirrored=False):
    depth = taps.shape[1]
    band[...] = jnp.zeros(band.shape, BF16)
    for tap in range(9):
        for c in range(3):
            block = taps[26 - 3 * tap - c].T if mirrored else taps[3 * tap + c]
            for o in range(2):
                band[tap, pl.ds((c + o) * C, depth), pl.ds(o * C, C)] = block


def convolve(even, odd, band):
    total = jnp.zeros((GROUP * 256, 2 * C), F32)
    for a in range(3):
        for b in range(3):
            total = total + jnp.dot(
                window(even, odd, a, b), band[3 * a + b], preferred_element_type=F32
            )
    return total


def add_taps(sums, slopes, even, odd):
    turned = slopes.astype(F32).T.astype(BF16)
    for a in range(3):
        for b in range(3):
            sums[3 * a + b] += jnp.dot(
                turned, window(even, odd, a, b), preferred_element_type=F32
            )


def gather_taps(sums, grad, depth, first):
    for tap in range(9):
        for c in range(3):
            part = (
                sums[tap, 0:C, c * C : (c + 1) * C]
                + sums[tap, C : 2 * C, (c + 1) * C : (c + 2) * C]
            )
            grad[pl.ds(first + (3 * tap + c) * depth, depth)] = part.T[0:depth].astype(BF16)


def groups(info, order, act, start, stop):
    def step(number, _):
        members = []
        for g in range(GROUP):
            position = number * GROUP + g
            place = order[position]
            slot = info[place]
            members.append((position, place, jnp.maximum(slot, 0), slot >= 0))
        act(number, members)
        return 0

    lax.fori_loop(start, stop, step, 0)


def all_groups(info, order, act):
    groups(info, order, act, 0, (order[32] + GROUP - 1) // GROUP)


def spread_mask(keep):
    blocks = []
    for j in range(4):
        pair = [jnp.broadcast_to(keep[:, 2 * j + o : 2 * j + o + 1], (64, C)) for o in range(2)]
        blocks.append(jnp.concatenate(pair, axis=1))
    return jnp.concatenate(blocks, axis=0)


def sigmoid(value):
    return 1.0 / (1.0 + jnp.exp(-value))


def first_kernel(
    info, order, own, x_halo, y_halo, c_halo, mask, taps, bias,
    vol, faces, corners, gates,
    wide, band, even, odd, sems,
):
    copies = open_volume(own, x_halo, wide, sems)
    fill_band(band, taps)
    vol[...] = jnp.zeros(vol.shape, BF16)
    faces[...] = jnp.zeros(faces.shape, BF16)

    def forward(number, members):
        for g, (_, place, _, _) in enumerate(members):
            cut_patch(wide, coords(place), even.at[g], odd.at[g])
        both = convolve(even, odd, band) + bias[...]
        for g, (position, place, slot, live) in enumerate(members):
            linear = both[256 * g : 256 * g + 256]
            keep = jnp.where(live, spread_mask(mask[slot]), 0.0)
            sig = sigmoid(linear)
            hidden = keep * (linear * sig)
            gates[position] = (keep * (sig * (1.0 + linear * (1.0 - sig)))).astype(BF16)
            for j in range(4):
                piece = hidden[64 * j : 64 * j + 64].reshape(8, 8, 2 * C)
                put(vol, faces, coords(place), 2 * C * j, piece)

    close_volume(y_halo, c_halo, wide, copies)
    all_groups(info, order, forward)
    put_corners(faces, corners)


def second_kernel(
    info, order, own, x_halo, y_halo, c_halo, mask, taps, bias, cots,
    vol, faces, corners, results, slopes,
    wide, band, even, odd, sems,
):
    copies = open_volume(own, x_halo, wide, sems)
    fill_band(band, taps)
    vol[...] = jnp.zeros(vol.shape, BF16)
    faces[...] = jnp.zeros(faces.shape, BF16)
    slopes[...] = jnp.zeros(slopes.shape, BF16)

    def forward(number, members):
        for g, (_, place, _, _) in enumerate(members):
            cut_patch(wide, coords(place), even.at[g], odd.at[g])
        both = convolve(even, odd, band) + bias[...]
        for g, (position, place, slot, live) in enumerate(members):
            worker = info[32 + slot]
            linear = both[256 * g : 256 * g + 256]
            keep = jnp.where(live, spread_mask(mask[slot]), 0.0)
            sig = sigmoid(linear)
            output = keep * (linear * sig)
            slope = keep * (sig * (1.0 + linear * (1.0 - sig)))
            for j in range(4):
                rows = slice(64 * j, 64 * j + 64)
                lanes = pl.ds(2 * C * j, 2 * C)
                piece = cots[worker, :, :, lanes].astype(F32).reshape(64, 2 * C) * slope[rows]
                slopes[position, pl.ds(64 * j, 64)] = piece.astype(BF16)
                put(vol, faces, coords(place), 2 * C * j, piece.reshape(8, 8, 2 * C))

            @pl.when(live)
            def _():
                for j in range(4):
                    rows = output[64 * j : 64 * j + 64].reshape(8, 8, 2 * C)
                    results[worker, :, :, pl.ds(2 * C * j, 2 * C)] = rows.astype(BF16)

    close_volume(y_halo, c_halo, wide, copies)
    all_groups(info, order, forward)
    put_corners(faces, corners)


def total_of(grads, final, base, parts, send, buffers):
    x, y = lax.axis_index("gx"), lax.axis_index("gy")
    core = lax.rem(y, 2)
    spot = {"x": x // 4, "z": lax.rem(x, 4), "y": y // 2}
    partner = (x, y + 1 - 2 * core)
    steps = range(1, 4)
    from_core, half, *part_buffers = buffers
    count = half.shape[0]
    mine, others = base + core * count, base + (1 - core) * count

    def peer(axis, k):
        at = lax.rem(spot[axis] + k, 4)
        if axis == "x":
            return at, (4 * at + spot["z"], y)
        if axis == "z":
            return at, (4 * spot["x"] + at, y)
        return at, (x, 2 * at + core)

    def rows(start, size):
        return pl.ds(pl.multiple_of(start, 16), size)

    flights = []
    for offset, size, _ in parts:
        source = grads.at[rows(others + offset, size)]
        flights.append([send(source, from_core.at[pl.ds(offset, size)], partner)])
    yield
    for p, (offset, size, axes) in enumerate(parts):
        finish(flights[p])
        here = pl.ds(offset, size)
        kept = grads[rows(mine + offset, size)].astype(F32)
        half[here] = (kept + from_core[here].astype(F32)).astype(BF16)
        flights[p] = []
        for k in steps:
            at, device = peer(axes[0], k)
            piece = half.at[rows(offset + at * (size // 4), size // 4)]
            flights[p].append(send(piece, part_buffers[4 * p].at[k - 1], device))
    yield
    for p, (offset, size, axes) in enumerate(parts):
        finish(flights[p])
        got, kept, _, _ = part_buffers[4 * p : 4 * p + 4]
        total = half[rows(offset + spot[axes[0]] * (size // 4), size // 4)].astype(F32)
        for k in steps:
            total = total + got[k - 1].astype(F32)
        kept[...] = total
        flights[p] = []
        for k in steps:
            at, device = peer(axes[1], k)
            piece = kept.at[rows(at * (size // 16), size // 16)]
            flights[p].append(send(piece, part_buffers[4 * p + 2].at[k - 1], device))
    yield
    for p, (offset, size, axes) in enumerate(parts):
        finish(flights[p])
        _, kept, got, line = part_buffers[4 * p : 4 * p + 4]
        total = kept[rows(spot[axes[1]] * (size // 16), size // 16)]
        for k in steps:
            total = total + got[k - 1]
        piece = line.at[spot[axes[2]]]
        piece[...] = total
        flights[p] = [send(piece, piece, peer(axes[2], k)[1]) for k in steps]
    yield
    for p, (offset, size, axes) in enumerate(parts):
        finish(flights[p])
        line = part_buffers[4 * p + 3]
        start = mine + offset + spot[axes[0]] * (size // 4) + spot[axes[1]] * (size // 16)
        here = rows(start, size // 16)
        final[here] = (line[0] + line[1] + line[2] + line[3]).astype(BF16)
        piece = final.at[here]
        flights[p] = [send(piece, piece, peer(axes[1], k)[1]) for k in steps]
    yield
    for p, (offset, size, axes) in enumerate(parts):
        finish(flights[p])
        piece = final.at[rows(mine + offset + spot[axes[0]] * (size // 4), size // 4)]
        flights[p] = [send(piece, piece, peer(axes[0], k)[1]) for k in steps]
    yield
    for p, (offset, size, axes) in enumerate(parts):
        finish(flights[p])
        piece = final.at[rows(mine + offset, size)]
        flights[p] = [send(piece, piece, partner)]
    yield
    for flight in flights:
        finish(flight)
    yield


def total_buffers(parts):
    count = sum(size for _, size, _ in parts)
    buffers = [pltpu.VMEM((count, C), BF16)] * 2
    for _, size, _ in parts:
        buffers.append(pltpu.VMEM((3, size // 4, C), BF16))
        buffers.append(pltpu.VMEM((size // 4, C), F32))
        buffers.append(pltpu.VMEM((3, size // 16, C), F32))
        buffers.append(pltpu.VMEM((4, size // 16, C), F32))
    return buffers


PARTS_ONE = ((0, 512, "xzy"), (512, 512, "zyx"), (1024, 512, "yxz"))
PARTS_TWO = ((0, 768, "zxy"), (768, 512, "xyz"), (1280, 512, "yzx"))
ROWS_ONE = 2 * 1536
ROWS_TWO = 2 * 1792


def third_kernel(
    info, order,
    vol, faces, corners, slopes_two,
    own_mid, x_halo_mid, y_halo_mid, c_halo_mid, own_in, x_halo_in, y_halo_in, c_halo_in,
    gates, taps, results, c_in,
    final, arrived,
    grads, wide, wide_other, band, even, odd, sums, slopes, y_halo, c_halo,
    send_sem, recv_sem, sems, sems_other, *buffers,
):
    x, y = lax.axis_index("gx"), lax.axis_index("gy")
    core, chip = lax.rem(y, 2), y // 2
    inner = pl.ds(C, LINE)
    x_halo = [wide.at[17 * end, pl.ds(1, 2), :, inner] for end in range(2)]
    plan = halo_plan((vol.at[0], vol.at[15]), faces, corners, x_halo, y_halo, c_halo)
    devices = [device for _, _, device in plan] + [(x, y + 1 - 2 * core)]
    for k in range(1, 4):
        devices.append((4 * lax.rem(x // 4 + k, 4) + lax.rem(x, 4), y))
        devices.append((4 * (x // 4) + lax.rem(x + k, 4), y))
        devices.append((x, 2 * lax.rem(chip + k, 4) + core))
    workers = [lax.rem(x + k, 16) for k in range(1, 16)]
    devices += [(worker, y) for worker in workers]
    loads_mid = open_volume(own_mid, x_halo_mid, wide_other, sems_other)
    loads = open_volume(vol, None, wide, sems)
    moves = [pltpu.make_async_copy(results.at[x], arrived.at[x], sems.at[1])]
    moves[0].start()
    greet(devices)
    send = sender_of(send_sem, recv_sem)
    halo = [send(*item) for item in plan]
    for worker in workers:
        moves.append(send(results.at[worker], arrived.at[x], (worker, y)))
    buffers_one, buffers_two = buffers[: len(buffers) // 2], buffers[len(buffers) // 2 :]
    total_one = total_of(grads, final, 0, PARTS_ONE, send, buffers_one)
    total_two = total_of(grads, final, ROWS_ONE, PARTS_TWO, send, buffers_two)
    count = 16 // GROUP

    def tap_sums(source):
        def act(number, members):
            for g, (_, place, _, _) in enumerate(members):
                cut_patch(wide_other, coords(place), even.at[g], odd.at[g])
            rows = source[pl.ds(number * GROUP, GROUP)].reshape(GROUP * 256, 2 * C)
            add_taps(sums, rows, even, odd)

        return act

    def back(number, members):
        for g, (_, place, _, _) in enumerate(members):
            cut_patch(wide, coords(place), even.at[g], odd.at[g])
        both = convolve(even, odd, band)
        for g, (position, _, _, live) in enumerate(members):
            rows = both[256 * g : 256 * g + 256] * gates[position].astype(F32)
            slopes[position] = jnp.where(live, rows, 0.0).astype(BF16)

    def clear(first, last):
        grads[first:last] = jnp.zeros((last - first, C), BF16)

    fill_band(band, taps, mirrored=True)
    sums[...] = jnp.zeros(sums.shape, F32)
    clear(27 * c_in, ROWS_ONE)
    clear(ROWS_ONE + 27 * C, ROWS_ONE + ROWS_TWO)
    close_volume(y_halo_mid, c_halo_mid, wide_other, loads_mid)
    groups(info, order, tap_sums(slopes_two), 0, count)
    gather_taps(sums, grads, C, ROWS_ONE)
    next(total_two)

    loads_in = open_volume(own_in, x_halo_in, wide_other, sems_other)
    sums[...] = jnp.zeros(sums.shape, F32)
    finish(halo)
    close_volume(y_halo, c_halo, wide, loads)
    groups(info, order, back, 0, count)
    next(total_two)
    close_volume(y_halo_in, c_halo_in, wide_other, loads_in)
    groups(info, order, tap_sums(slopes), 0, count)
    gather_taps(sums, grads, c_in, 0)
    for _ in range(6):
        next(total_one)
        next(total_two)
    next(total_one)
    next(total_one)
    finish(moves)


def finish_kernel(sender, grads, arrived, result, grad_one, grad_two):
    for number in range(result.shape[0]):
        result[number] = arrived[sender[number]]
    first = 0
    for out in (grad_one, grad_two):
        rows = grads[first : first + out.shape[0]].astype(F32)
        out[...] = rows * lax.rsqrt(jnp.mean(rows * rows) + 1e-05)
        first += ROWS_ONE


WIDE_SCRATCH = pltpu.VMEM((18, 4, 8, WIDE), BF16)
BAND_SCRATCH = pltpu.VMEM((9, 4 * C, 2 * C), BF16)
EVEN_SCRATCH = pltpu.VMEM((GROUP, 3, 80, PATCH), BF16)
ODD_SCRATCH = pltpu.VMEM((GROUP, 3, 64, PATCH), BF16)
SLOPES_SCRATCH = pltpu.VMEM((16, 256, 2 * C), BF16)
SUMS_SCRATCH = pltpu.VMEM((9, 2 * C, 4 * C), F32)
SEMS = pltpu.SemaphoreType.DMA((3,))
PARAMS = pltpu.CompilerParams(vmem_limit_bytes=LIMIT)


def body(
    features,
    voxel_mask,
    occupancy,
    send_counts,
    weight_one,
    bias_one,
    weight_two,
    bias_two,
    cotangent,
):
    c_in = weight_one.shape[1]
    mask = voxel_mask[0, 0].reshape(16, 64, 8).astype(F32)
    *vol_in, cots, info, order, sender = pl.pallas_call(
        volume_kernel,
        out_shape=(
            VOLUME,
            FACES,
            CORNERS,
            jax.ShapeDtypeStruct((16, 8, 8, BRICK), BF16),
            jax.ShapeDtypeStruct((49,), jnp.int32),
            jax.ShapeDtypeStruct((33,), jnp.int32),
            jax.ShapeDtypeStruct((9,), jnp.int32),
        ),
        in_specs=[SMEM, SMEM, VMEM, VMEM, VMEM],
        out_specs=(VMEM,) * 4 + (SMEM,) * 3,
        compiler_params=PARAMS,
        name="volume",
    )(occupancy, send_counts, features[0, 0], mask, cotangent[0, 0])
    halo_in = halo_exchange(*vol_in, 0)
    halo_in, cots = lax.optimization_barrier((halo_in, cots))
    cots = lax.all_to_all(cots, "gx", split_axis=0, concat_axis=0, tiled=True)

    *hidden, gates = pl.pallas_call(
        first_kernel,
        out_shape=(VOLUME, FACES, CORNERS, jax.ShapeDtypeStruct((16, 256, 2 * C), BF16)),
        in_specs=[SMEM, SMEM, ANY, ANY, VMEM, VMEM, VMEM, VMEM, VMEM],
        out_specs=(VMEM,) * 4,
        scratch_shapes=[WIDE_SCRATCH, BAND_SCRATCH, EVEN_SCRATCH, ODD_SCRATCH, SEMS],
        compiler_params=PARAMS,
        cost_estimate=pl.CostEstimate(flops=11 * 10**9, bytes_accessed=10**8, transcendentals=0),
        name="first",
    )(info, order, vol_in[0], *halo_in, mask, weight_one, jnp.tile(bias_one, 2)[None])
    halo_mid = halo_exchange(*hidden, 1)

    *edge, results, slopes = pl.pallas_call(
        second_kernel,
        out_shape=(
            VOLUME,
            FACES,
            CORNERS,
            jax.ShapeDtypeStruct((16, 8, 8, BRICK), BF16),
            jax.ShapeDtypeStruct((16, 256, 2 * C), BF16),
        ),
        in_specs=[SMEM, SMEM, ANY, ANY, VMEM, VMEM, VMEM, VMEM, VMEM, VMEM],
        out_specs=(VMEM,) * 5,
        scratch_shapes=[WIDE_SCRATCH, BAND_SCRATCH, EVEN_SCRATCH, ODD_SCRATCH, SEMS],
        compiler_params=PARAMS,
        name="second",
    )(info, order, hidden[0], *halo_mid, mask, weight_two, jnp.tile(bias_two, 2)[None], cots)
    grads, arrived = pl.pallas_call(
        lambda *refs: third_kernel(*refs[:17], c_in, *refs[17:]),
        out_shape=(
            jax.ShapeDtypeStruct((ROWS_ONE + ROWS_TWO, C), BF16),
            jax.ShapeDtypeStruct((16, 8, 8, BRICK), BF16),
        ),
        in_specs=[SMEM, SMEM, ANY, ANY, ANY, VMEM]
        + [ANY, ANY, VMEM, VMEM, ANY, ANY, VMEM, VMEM]
        + [VMEM, VMEM, ANY],
        out_specs=(VMEM, ANY),
        scratch_shapes=[
            pltpu.VMEM((ROWS_ONE + ROWS_TWO, C), BF16),
            WIDE_SCRATCH, WIDE_SCRATCH, BAND_SCRATCH, EVEN_SCRATCH, ODD_SCRATCH, SUMS_SCRATCH,
            SLOPES_SCRATCH, pltpu.VMEM(FACES.shape, BF16), pltpu.VMEM(CORNERS.shape, BF16),
            pltpu.SemaphoreType.DMA((128,)), pltpu.SemaphoreType.DMA((128,)), SEMS, SEMS,
            *total_buffers(PARTS_ONE), *total_buffers(PARTS_TWO),
        ],
        compiler_params=pltpu.CompilerParams(
            collective_id=3, has_side_effects=True, vmem_limit_bytes=LIMIT
        ),
        cost_estimate=pl.CostEstimate(flops=33 * 10**9, bytes_accessed=10**8, transcendentals=0),
        name="third",
    )(info, order, *edge, slopes, hidden[0], *halo_mid, vol_in[0], *halo_in, gates, weight_two, results)

    result, grad_one, grad_two = pl.pallas_call(
        finish_kernel,
        out_shape=(
            jax.ShapeDtypeStruct((8, 8, 8, BRICK), BF16),
            jax.ShapeDtypeStruct((27 * c_in, C), F32),
            jax.ShapeDtypeStruct((27 * C, C), F32),
        ),
        in_specs=[SMEM, VMEM, VMEM],
        out_specs=(VMEM,) * 3,
        compiler_params=PARAMS,
        name="finish",
    )(sender, grads, arrived)
    return (
        result[None, None],
        grad_one.reshape(weight_one.shape),
        grad_two.reshape(weight_two.shape),
    )


def solution(mesh):
    placed = (
        P("gx", "gy", None, None, None, None),
        P("gx", "gy", None, None),
        P("gx", "gy", None),
        P("gy", None, None),
        P(),
        P(),
        P(),
        P(),
        P("gx", "gy", None, None, None, None),
    )
    return jax.shard_map(
        body,
        mesh=mesh,
        in_specs=placed,
        out_specs=(P("gx", "gy", None, None, None, None), P(), P()),
        check_vma=False,
    )
```
